128 devices in a mesh: row: 4 (over z), kv: 32 (over x, y, core).
Axes of the slice: x: 4, y: 4, z: 4, core: 2. Of those that a mesh axis runs over, the one named last changes fastest.
Arguments:
- query: bfloat16 [8, 128, 576], P('row')
- latent_cache: bfloat16 [8, 163840, 576], P('row', 'kv')
- new_latent: bfloat16 [8, 576], P('row'), may hold values from -12 to 12
- lengths: int32 [8], P('row'), may hold values from 20480 to 163840, as said below
- w_uv: bfloat16 [128, 512, 128], P('kv'), may hold values from -0.25 to 0.25
- w_o: bfloat16 [16384, 7168], P('kv'), may hold values from -0.046875 to 0.046875
- hidden_in: bfloat16 [8, 7168], P('row'), may hold values from -0.59765625 to 0.59765625
- norm_gain: bfloat16 [7168], replicated, may hold values from 0.099609375 to 1.8984375
- w_gate: bfloat16 [7168, 18432], P(None, ('row', 'kv')), may hold values from -0.0625 to 0.0625
- w_up: bfloat16 [7168, 18432], P(None, ('row', 'kv')), may hold values from -0.0625 to 0.0625
- w_down: bfloat16 [18432, 7168], P(('row', 'kv')), may hold values from -0.15625 to 0.15625
Outputs:
- layer_out: float32 [8, 7168], P('row', 'kv')
The draws below stay inside these ranges and needn't reach their ends.
Inputs may be any that keep to these rules, and one draw needn't show every extreme that they name: `lengths`: each row's count of filled cache positions, each between 20480 and 163840; some row fills all 163840.
All inputs are finite; a program needn't handle non-finite values.
Results may differ from the reference program's by a relative error of at most 0.035.
Values may be sent and summed in bfloat16 or wider, within the bound.
A program may use at most 128 MiB of HBM per device.

```python
import jax
import jax.numpy as jnp
from jax import lax

HEADS = 128
LATENT = 512
ROPE = 64
HEAD_DIM = 128
D = 7168
FF = 18432
QK = 576
ROWS = 8
CAP = 163840


def draw_query(key, part):
    key = jax.random.fold_in(key, 11)
    base_key = jax.random.fold_in(key, 0)
    values = 1.5 * jnp.clip(jax.random.normal(base_key, (ROWS, HEADS, QK), jnp.float32), -6.0, 6.0)
    return values.astype(jnp.bfloat16)


def draw_latent_cache(key, part):
    key = jax.random.fold_in(key, 5)
    values = jnp.clip(jax.random.normal(key, (ROWS, CAP, QK), jnp.float32), -6.0, 6.0)
    return values.astype(jnp.bfloat16)


def draw_lengths(key, part):
    key = jax.random.fold_in(key, 3)
    first_key, second_key = jax.random.split(key)
    counts = jax.random.randint(first_key, (ROWS,), CAP // 8, CAP + 1)
    full_row = jax.random.randint(second_key, (), 0, ROWS)
    return jnp.where(jnp.arange(ROWS) == full_row, CAP, counts).astype(jnp.int32)


def with_spikes(values, stream_key, source, target, shards_of, factor):
    def block_of(dim):
        return (jnp.arange(values.shape[dim]) // (values.shape[dim] // shards_of)).reshape((-1,) + (1,) * (values.ndim - 1 - dim))

    one_side = jax.random.permutation(stream_key, shards_of)[block_of(target)]
    far = (block_of(target) + shards_of // 2) % shards_of
    return jnp.where((block_of(source) == one_side) | (block_of(source) == far), factor * values, values)


def block_levels(stream_key, shape, pieces, smallest, largest):
    gain = 1.0
    for position, blocks in pieces:
        steps = jax.random.uniform(jax.random.fold_in(jax.random.fold_in(stream_key, 6), position), (blocks,), jnp.float32, smallest / len(pieces), largest / len(pieces))
        gain = gain * jnp.repeat(jnp.exp(steps), shape[position] // blocks).reshape((-1,) + (1,) * (len(shape) - 1 - position))
    return gain


def noise(stream_key, shape, deviation, bound, shards=(), held_as=jnp.bfloat16):
    loudness = block_levels(stream_key, shape, shards, -0.22, 0.18) if shards else 1.0
    values = jax.random.normal(stream_key, shape, jnp.float32) * deviation * loudness
    return jnp.minimum(jnp.maximum(values, -bound), bound).astype(held_as)


def gaussian_with(stream_key, dims, spread, bound, shards, heavy, kind=jnp.bfloat16):
    values = spread * jax.random.normal(stream_key, dims, jnp.float32)
    if shards:
        values = values * block_levels(stream_key, dims, shards, -0.22, 0.18)
    return jnp.clip(with_spikes(values, jax.random.fold_in(stream_key, 3), *heavy), -bound, bound).astype(kind)


def setup_inputs(seed: int = 0) -> dict:
    arg_keys = jax.random.split(jax.random.key(seed), 12)
    return {
        "query": draw_query(jax.random.fold_in(arg_keys[11], 71), 0),
        "latent_cache": draw_latent_cache(jax.random.fold_in(arg_keys[11], 71), 0),
        "new_latent": noise(arg_keys[2], (ROWS, QK), 2.0, 12.0, ((0, 4),)),
        "lengths": draw_lengths(jax.random.fold_in(arg_keys[11], 71), 0),
        "w_uv": noise(arg_keys[4], (HEADS, LATENT, HEAD_DIM), LATENT ** -0.5, 0.25, ((0, 32),)),
        "w_o": noise(arg_keys[5], (HEADS * HEAD_DIM, D), (HEADS * HEAD_DIM) ** -0.5, 0.046875, ((0, 32),)),
        "hidden_in": noise(arg_keys[6], (ROWS, D), 0.1, 0.59765625, ((0, 4),)),
        "norm_gain": jnp.clip(1.0 + 0.18 * jax.random.normal(arg_keys[7], (D,), jnp.float32), 0.099609375, 1.8984375).astype(jnp.bfloat16),
        "w_gate": noise(arg_keys[8], (D, FF), D ** -0.5, 0.0625, ((1, 128),)),
        "w_up": noise(arg_keys[9], (D, FF), D ** -0.5, 0.0625, ((1, 128),)),
        "w_down": gaussian_with(arg_keys[10], (FF, D), FF ** -0.5, 0.15625, ((0, 128),), (0, 1, 128, 5.5)),
    }


NEG_FILL = -1e+30

def one_row(items):
    query_row, cache_row, new_row, length = items
    score_scale = (HEAD_DIM + ROPE) ** (-0.5)
    scores = jnp.dot(query_row, cache_row.T, preferred_element_type=jnp.float32) * score_scale
    new_score = jnp.dot(query_row, new_row, preferred_element_type=jnp.float32) * score_scale
    valid = (jnp.arange(CAP) < length)[None, :]
    top_score = jnp.maximum(lax.optimization_barrier(jnp.max(jnp.where(valid, scores, NEG_FILL), axis=1)), new_score)
    weights = jnp.where(valid, jnp.exp(scores - top_score[:, None]), 0.0).astype(jnp.bfloat16)
    own_weight = jnp.exp(new_score - top_score)
    total = lax.optimization_barrier(jnp.sum(weights.astype(jnp.float32), axis=1)) + own_weight
    weighted = jnp.dot(weights, cache_row[:, :LATENT], preferred_element_type=jnp.float32)
    weighted = weighted + own_weight[:, None] * new_row[:LATENT].astype(jnp.float32)[None, :]
    return (weighted / total[:, None]).astype(jnp.bfloat16)

def reference(query, latent_cache, new_latent, lengths, w_uv, w_o, hidden_in, norm_gain, w_gate, w_up, w_down):
    attended = lax.map(one_row, (query, latent_cache, new_latent, lengths))
    head_values = jnp.einsum('rhl,hld->rhd', attended.astype(jnp.float32), w_uv.astype(jnp.float32)).astype(jnp.bfloat16)
    flat_values = head_values.reshape(ROWS, HEADS * HEAD_DIM)
    attn = jnp.dot(flat_values, w_o, preferred_element_type=jnp.float32)
    stream = (hidden_in.astype(jnp.float32) + attn).astype(jnp.bfloat16)
    stream_f = stream.astype(jnp.float32)
    mean_sq = lax.optimization_barrier(jnp.mean(stream_f * stream_f, axis=1, keepdims=True))
    normed = (stream_f * lax.rsqrt(mean_sq + 1e-06) * norm_gain.astype(jnp.float32)[None, :]).astype(jnp.bfloat16)
    gate_proj = jnp.dot(normed, w_gate, preferred_element_type=jnp.float32)
    up_proj = jnp.dot(normed, w_up, preferred_element_type=jnp.float32)
    hidden = (jax.nn.silu(gate_proj) * up_proj).astype(jnp.bfloat16)
    down_proj = jnp.dot(hidden, w_down, preferred_element_type=jnp.float32)
    return (stream_f + down_proj).astype(jnp.float32)
```

```python
import jax
import jax.numpy as jnp
from jax import lax
from jax.experimental import pallas as pl
from jax.experimental.pallas import tpu as pltpu
from jax.sharding import PartitionSpec as P

LOGICAL = pl.DeviceIdType.LOGICAL
F32, BF16 = jnp.float32, jnp.bfloat16

HEADS, LATENT, ROPE, HEAD_DIM, QK = 128, 512, 64, 128, 576
D, LOCAL_FF, SPAN = 7168, 144, 5120
KV, ROWS, HERE = 32, 4, 2
OUT_COLS = D // KV
CHUNK = 1024
CHUNKS = SPAN // CHUNK
REDUCERS = 14
LOG2E = 1.4426950408889634
SCALE2 = LOG2E * (HEAD_DIM + ROPE) ** -0.5
NEG_FILL = -1e30


def dot(a, b, dims=((1,), (0,))):
    return lax.dot_general(a, b, (dims, ((), ())), preferred_element_type=F32)


def kernel(
    q_hbm, cache_hbm, new_hbm, lengths_ref, uv_hbm, wo_hbm, hid_hbm, gain_hbm, gate_hbm, up_hbm, down_hbm,
    out_ref,
    qt, kt, new, uv, wo, hid_in, gain, wg, wu, wd,
    q, s, w, acc, hid_tiles,
    part_out, part_in, attn_out, attn_in, row_tiles, stream_own, stream_all, wide,
    down_out, down_in, last_own, last_in, wide_stream,
    in_sem, cache_sem, send_sem, recv_sem,
):
    k = lax.axis_index("kv")
    z = lax.axis_index("row")

    small = [
        pltpu.make_async_copy(src, dst, in_sem.at[i])
        for i, (src, dst) in enumerate(((q_hbm, qt), (new_hbm, new), (hid_hbm, hid_in), (gain_hbm, gain)))
    ]
    for copy in small:
        copy.start()
    cache = [
        [
            pltpu.make_async_copy(
                cache_hbm.at[r, :, pl.ds(c * CHUNK, CHUNK)], kt.at[r, :, pl.ds(c * CHUNK, CHUNK)], cache_sem.at[r, c]
            )
            for c in range(CHUNKS)
        ]
        for r in range(HERE)
    ]
    for r in range(HERE):
        for c in range(CHUNKS):
            cache[r][c].start()
    weights = [
        pltpu.make_async_copy(src, dst, in_sem.at[4 + i])
        for i, (src, dst) in enumerate(((uv_hbm, uv), (wo_hbm, wo), (gate_hbm, wg), (up_hbm, wu), (down_hbm, wd)))
    ]

    barrier = pltpu.get_barrier_semaphore()

    plane = z * KV
    own_chip, own_core = lax.div(k, 2), lax.rem(k, 2)
    xs = [4 * lax.rem(lax.div(own_chip, 4) + d, 4) for d in range(4)]
    ys = [lax.rem(lax.rem(own_chip, 4) + d, 4) for d in range(4)]
    cores = [own_core, 1 - own_core]
    offsets = sorted(((dx, dy) for dx in range(4) for dy in range(4)), key=lambda o: -min(o[0], 4 - o[0]) - min(o[1], 4 - o[1]))
    chips = [xs[dx] + ys[dy] for dx, dy in offsets]
    peers = [2 * chip + core for chip in chips for core in cores]
    del peers[-2]
    row_peers = [lax.rem(z + d, ROWS) * KV + k for d in (2, 1, 3)]
    for peer in [plane + p for p in peers] + row_peers:
        pl.semaphore_signal(barrier, inc=1, device_id=peer, device_id_type=LOGICAL)

    def send(src, dst, lane, device):
        pltpu.make_async_remote_copy(
            src_ref=src, dst_ref=dst, send_sem=send_sem.at[lane], recv_sem=recv_sem.at[lane],
            device_id=device, device_id_type=LOGICAL,
        ).start()

    def send_kv(src, dst, lane):
        for peer in peers:
            send(src(peer), dst, lane, plane + peer)

    def send_row(src, dst, lane):
        for peer in row_peers:
            send(src, dst, lane, peer)

    def wait_for(sem, buffer, count):
        span = buffer.at[pl.ds(0, count)]
        pltpu.make_async_copy(span, span, sem).wait()

    sub = lax.broadcasted_iota(jnp.int32, (8, 128), 0)
    lane = lax.broadcasted_iota(jnp.int32, (8, 128), 1)

    for copy in small:
        copy.wait()
    new_score = []
    for r in range(HERE):
        q_f = qt[r].astype(F32).T
        q[r] = q_f.astype(BF16)
        new_score.append(jnp.sum(q_f * new[r : r + 1, :].astype(F32), axis=1, keepdims=True) * SCALE2)
    def packed(rows, j):
        base = 512 * j
        tile = rows[:, base : base + 128]
        for c in range(1, 4):
            tile = jnp.where(sub // 2 == c, rows[:, base + 128 * c : base + 128 * (c + 1)], tile)
        return tile

    position = lax.broadcasted_iota(jnp.int32, (1, CHUNK), 1) + k * SPAN

    def scores(r, c):
        cache[r][c].wait()
        cols = pl.ds(c * CHUNK, CHUNK)
        raw = dot(q[r], kt[r, :, cols]) * SCALE2
        raw = jnp.where(position + c * CHUNK < lengths_ref[r], raw, NEG_FILL)
        s[r, :, cols] = raw
        return jnp.max(raw, axis=1, keepdims=True)

    def weigh(r, c, top):
        cols = pl.ds(c * CHUNK, CHUNK)
        value = jnp.exp2(s[r, :, cols] - top)
        w[r, :, cols] = value.astype(BF16)
        return jnp.sum(value, axis=1, keepdims=True)

    def pv(r, c):
        cols = pl.ds(c * CHUNK, CHUNK)
        part = dot(w[r, :, cols], kt[r, :LATENT, cols], ((1,), (1,)))
        if c == 0:
            acc[r] = part
        else:
            acc[r] += part

    top = list(new_score)
    total = [jnp.zeros((HEADS, 1), F32)] * HERE
    for c in range(CHUNKS):
        top[0] = jnp.maximum(top[0], scores(0, c))
    weights[0].start()
    weights[1].start()
    for c in range(CHUNKS):
        top[1] = jnp.maximum(top[1], scores(1, c))
        total[0] = total[0] + weigh(0, c, top[0])
    for copy in weights[2:]:
        copy.start()
    for c in range(CHUNKS):
        pv(0, c)
        total[1] = total[1] + weigh(1, c, top[1])
    for c in range(CHUNKS):
        pv(1, c)

    half = lax.broadcasted_iota(jnp.int32, (16, 8, 128), 1) < 4
    left = lax.broadcasted_iota(jnp.int32, (HEADS, 128), 1) < 64
    wide_zero = jnp.zeros((HEADS, 128), F32)

    def share(first, second):
        t0, t1 = first.reshape(16, 8, 128), second.reshape(16, 8, 128)
        return jnp.where(half, t0, pltpu.roll(t1, 4, 1)), jnp.where(half, pltpu.roll(t0, 4, 1), t1)

    def rounded(value):
        return value.astype(BF16).astype(F32)

    logs = []
    for r in range(HERE):
        own_new = jnp.where(k == 0, jnp.exp2(new_score[r] - top[r]), 0.0)
        norm = jnp.maximum(total[r] + own_new, 1e-30)
        log_total = top[r] + jnp.log(norm) * LOG2E
        high = rounded(log_total)
        middle = rounded(log_total - high)
        low = log_total - high - middle
        logs.append(share(jnp.where(left, high, middle), jnp.where(left, low, wide_zero)))
        mine = (acc[r] + own_new * new[r : r + 1, :LATENT].astype(F32)) * (1.0 / norm)
        quarters = [mine[:, 128 * c : 128 * c + 128] for c in range(4)]
        both = [share(quarters[2 * u], quarters[2 * u + 1]) for u in range(2)]
        for core in range(2):
            part_out[:, core, r] = jnp.concatenate([both[0][core], both[1][core]], axis=1).astype(BF16)
    for core in range(2):
        part_out[:, core, HERE] = jnp.concatenate([logs[0][core], logs[1][core]], axis=1).astype(BF16)
    pl.semaphore_wait(barrier, KV - 1 + ROWS - 1)
    send_kv(lambda peer: part_out.at[lax.div(peer, 2), lax.rem(peer, 2)], part_in.at[k], 1)
    part_in[k] = part_out[own_chip, own_core]

    hid_f = hid_in[...].astype(F32)
    hid_rows = jnp.where(lax.broadcasted_iota(jnp.int32, (8, D), 0) % 2 == 0, hid_f[0:1], hid_f[1:2])

    for j in range(REDUCERS):
        hid_tiles[j] = packed(hid_rows, j)

    wait_for(recv_sem.at[1], part_in, KV - 1)
    weights[0].wait()
    att = []
    for r in range(HERE):
        log_parts = part_in[:, HERE, 8 * r : 8 * r + 8].astype(F32)
        log_parts = log_parts + pltpu.roll(log_parts, 64, 2)
        log_parts = log_parts + pltpu.roll(log_parts, 4, 1)
        factor = jnp.exp2(log_parts - jnp.max(log_parts, axis=0)[None])
        factor = factor * (1.0 / jnp.sum(factor, axis=0))[None]
        data = part_in[:, r].astype(F32)
        att.append([jnp.sum(data[:, 8 * u : 8 * u + 8] * factor, axis=0) for u in range(2)])
    pieces = []
    for c in range(4):
        lo, hi = att[0][c // 2], att[1][c // 2]
        if c % 2 == 0:
            pieces.append(jnp.where(sub < 4, lo, pltpu.roll(hi, 4, 0)))
        else:
            pieces.append(jnp.where(sub < 4, pltpu.roll(lo, 4, 0), hi))
    attended = jnp.concatenate(pieces, axis=1).astype(BF16)
    values = []
    for h in range(4):
        got = dot(attended, uv[h])
        values.append(jnp.where(sub % 2 == 0, got[h : h + 1], got[4 + h : 5 + h]))
    head_values = jnp.concatenate(values, axis=1).astype(BF16)
    weights[1].wait()
    partial = dot(head_values, wo[...])
    for j in range(REDUCERS):
        attn_out[j] = packed(partial, j)

    for chip in chips:

        @pl.when(jnp.logical_and(chip < REDUCERS, k != 2 * chip))
        def _(chip=chip):
            send(attn_out.at[chip], attn_in.at[k], 2, plane + 2 * chip)

    reducer = jnp.logical_and(k % 2 == 0, k < 2 * REDUCERS)

    @pl.when(reducer)
    def _():
        j = own_chip
        attn_in[k] = attn_out[j]
        own_hid = hid_tiles[j]
        wait_for(recv_sem.at[2], attn_in, KV - 1)
        mine = (jnp.sum(attn_in[...], axis=0) + own_hid).astype(BF16).astype(F32)
        row_tiles[z] = mine
        stream_own[...] = mine
        send_row(stream_own, row_tiles.at[z], 3)
        wait_for(recv_sem.at[3], row_tiles, ROWS - 1)
        tiles = []
        for c in range(4):
            tile = None
            for zz in range(ROWS):
                shift = (2 * zz - 2 * c) % 8
                piece = row_tiles[zz]
                if shift:
                    piece = pltpu.roll(piece, shift, 0)
                tile = piece if tile is None else jnp.where(sub // 2 == zz, piece, tile)
            tiles.append(tile)
        for u in range(2):
            both = jnp.concatenate(tiles[2 * u : 2 * u + 2], axis=0).astype(BF16)
            wide[u] = both
            stream_all[j, u] = both
        send_kv(lambda peer: wide, stream_all.at[j], 4)
        wait_for(recv_sem.at[4], stream_all, REDUCERS - 1)

    @pl.when(jnp.logical_not(reducer))
    def _():
        wait_for(recv_sem.at[4], stream_all, REDUCERS)

    parts = stream_all[...].astype(F32)
    stream = jnp.concatenate(
        [parts[t // 4, (t // 2) % 2, 8 * (t % 2) : 8 * (t % 2) + 8] for t in range(D // 128)], axis=1
    )
    mean_sq = jnp.sum(stream * stream, axis=1, keepdims=True) * (1.0 / D)
    normed = (stream * lax.rsqrt(mean_sq + 1e-06) * gain[...].astype(F32).reshape(1, D)).astype(BF16)
    for copy in weights[2:4]:
        copy.wait()
    gate_proj = dot(normed, wg[...], ((1,), (1,)))
    up_proj = dot(normed, wu[...], ((1,), (1,)))
    hidden = (gate_proj / (1.0 + jnp.exp(-gate_proj)) * up_proj).astype(BF16)
    weights[4].wait()
    down = dot(hidden, wd[...])
    down = jnp.concatenate([down, jnp.zeros((8, 128), F32)], axis=1)
    for p in range(KV):
        tile, shift = divmod(OUT_COLS * p, 128)
        three = [down[:, 128 * (tile + i) : 128 * (tile + i + 1)] for i in range(3)]
        if shift:
            turned = [pltpu.roll(t, 128 - shift, 1) for t in three]
            two = [jnp.where(lane < 128 - shift, turned[i], turned[i + 1]) for i in range(2)]
        else:
            two = three[:2]
        down_out[p] = jnp.concatenate(two, axis=0).astype(BF16)
    down_in[k] = down_out[k]
    send_kv(lambda peer: down_out.at[peer], down_in.at[k], 5)

    own_tile = lax.div(7 * k, 4)
    wide_stream[:, pl.ds(0, D)] = stream
    wide_stream[:, pl.ds(D, 512)] = jnp.zeros((8, 512), F32)
    own_stream = wide_stream[:, pl.ds(pl.multiple_of(own_tile * 128, 128), 512)]
    own_stream = pltpu.roll(own_stream, lax.rem(512 - (OUT_COLS * k - 128 * own_tile), 512), 1)[:, :256]

    wait_for(recv_sem.at[5], down_in, KV - 1)
    mine = jnp.sum(down_in[...].astype(F32), axis=0)
    last_own[...] = mine
    last_in[z] = mine
    send_row(last_own, last_in.at[z], 6)
    wait_for(recv_sem.at[6], last_in, ROWS - 1)
    summed = jnp.sum(last_in[...], axis=0)
    result = jnp.concatenate([summed[0:8], summed[8:16]], axis=1) + own_stream
    own = result[0:2]
    for zz in range(1, ROWS):
        own = jnp.where(z == zz, result[2 * zz : 2 * zz + 2], own)
    out_ref[...] = own[:, :OUT_COLS]

    for i, buffer in ((1, part_in), (5, down_in)):
        wait_for(send_sem.at[i], buffer, KV - 1)
    wait_for(send_sem.at[6], last_in, ROWS - 1)

    @pl.when(reducer)
    def _():
        wait_for(send_sem.at[2], attn_out, REDUCERS - 1)
        wait_for(send_sem.at[3], row_tiles, ROWS - 1)
        sent = s.at[0, pl.ds(0, 16), pl.ds(0, 128 * (KV - 1))]
        pltpu.make_async_copy(sent, sent, send_sem.at[4]).wait()

    @pl.when(jnp.logical_not(reducer))
    def _():
        wait_for(send_sem.at[2], attn_out, REDUCERS)


def body(query, latent_cache, new_latent, lengths, w_uv, w_o, hidden_in, norm_gain, w_gate, w_up, w_down):
    anywhere = pl.BlockSpec(memory_space=pl.ANY)
    vmem = pltpu.VMEM
    return pl.pallas_call(
        kernel,
        out_shape=jax.ShapeDtypeStruct((HERE, OUT_COLS), F32),
        in_specs=[anywhere] * 3 + [pl.BlockSpec(memory_space=pltpu.SMEM)] + [anywhere] * 7,
        out_specs=pl.BlockSpec(memory_space=vmem),
        scratch_shapes=[
            vmem((HERE, QK, HEADS), BF16),
            vmem((HERE, QK, SPAN), BF16),
            vmem((HERE, QK), BF16),
            vmem((4, LATENT, HEAD_DIM), BF16),
            vmem((4 * HEAD_DIM, D), BF16),
            vmem((HERE, D), BF16),
            vmem((D,), BF16),
            vmem((LOCAL_FF, D), BF16),
            vmem((LOCAL_FF, D), BF16),
            vmem((LOCAL_FF, D), BF16),
            vmem((HERE, HEADS, QK), BF16),
            vmem((HERE, HEADS, SPAN), F32),
            vmem((HERE, HEADS, SPAN), BF16),
            vmem((HERE, HEADS, LATENT), F32),
            vmem((REDUCERS, 8, 128), F32),
            vmem((KV // 2, 2, HERE + 1, 16, 128), BF16),
            vmem((KV, HERE + 1, 16, 128), BF16),
            vmem((REDUCERS, 8, 128), F32),
            vmem((KV, 8, 128), F32),
            vmem((ROWS, 8, 128), F32),
            vmem((8, 128), F32),
            vmem((REDUCERS, 2, 16, 128), BF16),
            vmem((2, 16, 128), BF16),
            vmem((KV, 16, 128), BF16),
            vmem((KV, 16, 128), BF16),
            vmem((16, 128), F32),
            vmem((ROWS, 16, 128), F32),
            vmem((8, D + 512), F32),
            pltpu.SemaphoreType.DMA((9,)),
            pltpu.SemaphoreType.DMA((HERE, CHUNKS)),
            pltpu.SemaphoreType.DMA((7,)),
            pltpu.SemaphoreType.DMA((7,)),
        ],
        compiler_params=pltpu.CompilerParams(
            collective_id=0, has_side_effects=True, vmem_limit_bytes=60 * 1024 * 1024
        ),
    )(
        jnp.swapaxes(query, 1, 2),
        jnp.swapaxes(latent_cache, 1, 2),
        new_latent,
        lengths,
        w_uv,
        w_o,
        hidden_in,
        norm_gain,
        w_gate.T,
        w_up.T,
        w_down,
    )


def solution(mesh):
    placed = (
        P("row", None, None),
        P("row", "kv", None),
        P("row", None),
        P("row"),
        P("kv", None, None),
        P("kv", None),
        P("row", None),
        P(),
        P(None, ("row", "kv")),
        P(None, ("row", "kv")),
        P(("row", "kv"), None),
    )
    return jax.shard_map(body, mesh=mesh, in_specs=placed, out_specs=P("row", "kv"), check_vma=False)
```

```python
import jax
import jax.numpy as jnp
from jax import lax
from jax.experimental import pallas as pl
from jax.experimental.pallas import tpu as pltpu
from jax.sharding import PartitionSpec as P

LOGICAL = pl.DeviceIdType.LOGICAL
F32, BF16 = jnp.float32, jnp.bfloat16

HEADS, LATENT, ROPE, HEAD_DIM, QK = 128, 512, 64, 128, 576
D, LOCAL_FF, SPAN = 7168, 144, 5120
KV, ROWS, HERE = 32, 4, 2
OUT_COLS = D // KV
CHUNK = 1024
BLOCK = 256
CHUNKS = SPAN // CHUNK
REDUCERS = 14
LOG2E = 1.4426950408889634
SCALE2 = LOG2E * (HEAD_DIM + ROPE) ** -0.5
NEG_FILL = -1e30


def dot(a, b, dims=((1,), (0,))):
    return lax.dot_general(a, b, (dims, ((), ())), preferred_element_type=F32)


def kernel(
    q_hbm, cache_hbm, new_hbm, lengths_ref, uv_hbm, wo_hbm, hid_hbm, gain_hbm, gate_hbm, up_hbm, down_hbm,
    out_ref,
    qt, kt, new, uv, wo, hid_in, gain, wg, wu, wd,
    q, s, w, acc, hid_tiles,
    part_out, part_in, attn_out, attn_in, row_tiles, stream_own, stream_all, wide,
    down_out, down_in, last_own, last_in, wide_stream,
    in_sem, cache_sem, send_sem, recv_sem,
):
    k = lax.axis_index("kv")
    z = lax.axis_index("row")

    small = [
        pltpu.make_async_copy(src, dst, in_sem.at[i])
        for i, (src, dst) in enumerate(((q_hbm, qt), (new_hbm, new), (hid_hbm, hid_in), (gain_hbm, gain)))
    ]
    for copy in small:
        copy.start()
    cache = [
        [
            pltpu.make_async_copy(
                cache_hbm.at[r, :, pl.ds(c * CHUNK, CHUNK)], kt.at[r, :, pl.ds(c * CHUNK, CHUNK)], cache_sem.at[r, c]
            )
            for c in range(CHUNKS)
        ]
        for r in range(HERE)
    ]
    for r in range(HERE):
        for c in range(CHUNKS):
            cache[r][c].start()
    weights = [
        pltpu.make_async_copy(src, dst, in_sem.at[4 + i])
        for i, (src, dst) in enumerate(((uv_hbm, uv), (wo_hbm, wo), (gate_hbm, wg), (up_hbm, wu), (down_hbm, wd)))
    ]

    barrier = pltpu.get_barrier_semaphore()

    plane = z * KV
    own_chip, own_core = lax.div(k, 2), lax.rem(k, 2)
    xs = [4 * lax.rem(lax.div(own_chip, 4) + d, 4) for d in range(4)]
    ys = [lax.rem(lax.rem(own_chip, 4) + d, 4) for d in range(4)]
    cores = [own_core, 1 - own_core]
    offsets = sorted(((dx, dy) for dx in range(4) for dy in range(4)), key=lambda o: -min(o[0], 4 - o[0]) - min(o[1], 4 - o[1]))
    chips = [xs[dx] + ys[dy] for dx, dy in offsets]
    peers = [2 * chip + core for chip in chips for core in cores]
    del peers[-2]
    row_peers = [lax.rem(z + d, ROWS) * KV + k for d in (2, 1, 3)]
    for peer in [plane + p for p in peers] + row_peers:
        pl.semaphore_signal(barrier, inc=1, device_id=peer, device_id_type=LOGICAL)

    def send(src, dst, lane, device):
        pltpu.make_async_remote_copy(
            src_ref=src, dst_ref=dst, send_sem=send_sem.at[lane], recv_sem=recv_sem.at[lane],
            device_id=device, device_id_type=LOGICAL,
        ).start()

    def send_kv(src, dst, lane):
        for peer in peers:
            send(src(peer), dst, lane, plane + peer)

    def send_row(src, dst, lane):
        for peer in row_peers:
            send(src, dst, lane, peer)

    def wait_for(sem, buffer, count):
        span = buffer.at[pl.ds(0, count)]
        pltpu.make_async_copy(span, span, sem).wait()

    sub = lax.broadcasted_iota(jnp.int32, (8, 128), 0)
    lane = lax.broadcasted_iota(jnp.int32, (8, 128), 1)

    small[0].wait()
    for r in range(HERE):
        q[r] = qt[r].astype(F32).T.astype(BF16)

    def packed(rows, j):
        base = 512 * j
        tile = rows[:, base : base + 128]
        for c in range(1, 4):
            tile = jnp.where(sub // 2 == c, rows[:, base + 128 * c : base + 128 * (c + 1)], tile)
        return tile

    position = lax.broadcasted_iota(jnp.int32, (1, BLOCK), 1) + k * SPAN

    def scores(r, c):
        cache[r][c].wait()
        most = None
        for first in range(c * CHUNK, (c + 1) * CHUNK, BLOCK):
            cols = pl.ds(first, BLOCK)
            raw = dot(q[r], kt[r, :, cols]) * SCALE2
            raw = jnp.where(position + first < lengths_ref[r], raw, NEG_FILL)
            s[r, :, cols] = raw
            for part in range(0, BLOCK, 128):
                piece = raw[:, part : part + 128]
                most = piece if most is None else jnp.maximum(most, piece)
        return most

    def weigh(r, c, top):
        cols = pl.ds(c * CHUNK, CHUNK)
        value = jnp.exp2(s[r, :, cols] - top)
        w[r, :, cols] = value.astype(BF16)
        added = value[:, :128]
        for part in range(128, CHUNK, 128):
            added = added + value[:, part : part + 128]
        return added

    def highest(r, parts):
        most = parts[0]
        for part in parts[1:]:
            most = jnp.maximum(most, part)
        new_score = jnp.sum(q[r].astype(F32) * new[r : r + 1, :].astype(F32), axis=1, keepdims=True) * SCALE2
        return new_score, jnp.maximum(jnp.max(most, axis=1, keepdims=True), new_score)

    def summed(parts):
        added = parts[0]
        for part in parts[1:]:
            added = added + part
        return jnp.sum(added, axis=1, keepdims=True)

    parts = [scores(0, c) for c in range(CHUNKS)]
    small[1].wait()
    new0, top0 = highest(0, parts)
    weights[0].start()
    weights[1].start()
    parts, sums = [], []
    for c in range(CHUNKS):
        parts.append(scores(1, c))
        sums.append(weigh(0, c, top0))
    for copy in weights[2:]:
        copy.start()
    new1, top1 = highest(1, parts)
    new_score, top = [new0, new1], [top0, top1]
    total = [summed(sums), summed([weigh(1, c, top1) for c in range(CHUNKS)])]
    for r in range(HERE):
        acc[r] = dot(w[r], kt[r, :LATENT, :], ((1,), (1,)))

    half = lax.broadcasted_iota(jnp.int32, (16, 8, 128), 1) < 4
    left = lax.broadcasted_iota(jnp.int32, (HEADS, 128), 1) < 64
    wide_zero = jnp.zeros((HEADS, 128), F32)

    def share(first, second):
        t0, t1 = first.reshape(16, 8, 128), second.reshape(16, 8, 128)
        return jnp.where(half, t0, pltpu.roll(t1, 4, 1)), jnp.where(half, pltpu.roll(t0, 4, 1), t1)

    def rounded(value):
        return value.astype(BF16).astype(F32)

    logs = []
    for r in range(HERE):
        own_new = jnp.where(k == 0, jnp.exp2(new_score[r] - top[r]), 0.0)
        norm = jnp.maximum(total[r] + own_new, 1e-30)
        log_total = top[r] + jnp.log(norm) * LOG2E
        high = rounded(log_total)
        middle = rounded(log_total - high)
        low = log_total - high - middle
        logs.append(share(jnp.where(left, high, middle), jnp.where(left, low, wide_zero)))
        mine = (acc[r] + own_new * new[r : r + 1, :LATENT].astype(F32)) * (1.0 / norm)
        quarters = [mine[:, 128 * c : 128 * c + 128] for c in range(4)]
        both = [share(quarters[2 * u], quarters[2 * u + 1]) for u in range(2)]
        for core in range(2):
            part_out[:, core, r] = jnp.concatenate([both[0][core], both[1][core]], axis=1).astype(BF16)
    for core in range(2):
        part_out[:, core, HERE] = jnp.concatenate([logs[0][core], logs[1][core]], axis=1).astype(BF16)
    pl.semaphore_wait(barrier, KV - 1 + ROWS - 1)
    send_kv(lambda peer: part_out.at[lax.div(peer, 2), lax.rem(peer, 2)], part_in.at[k], 1)
    part_in[k] = part_out[own_chip, own_core]

    for copy in small[2:]:
        copy.wait()
    hid_f = hid_in[...].astype(F32)
    hid_rows = jnp.where(lax.broadcasted_iota(jnp.int32, (8, D), 0) % 2 == 0, hid_f[0:1], hid_f[1:2])

    for j in range(REDUCERS):
        hid_tiles[j] = packed(hid_rows, j)

    wait_for(recv_sem.at[1], part_in, KV - 1)
    weights[0].wait()
    att = []
    for r in range(HERE):
        log_parts = part_in[:, HERE, 8 * r : 8 * r + 8].astype(F32)
        log_parts = log_parts + pltpu.roll(log_parts, 64, 2)
        log_parts = log_parts + pltpu.roll(log_parts, 4, 1)
        factor = jnp.exp2(log_parts - jnp.max(log_parts, axis=0)[None])
        factor = factor * (1.0 / jnp.sum(factor, axis=0))[None]
        data = part_in[:, r].astype(F32)
        att.append([jnp.sum(data[:, 8 * u : 8 * u + 8] * factor, axis=0) for u in range(2)])
    pieces = []
    for c in range(4):
        lo, hi = att[0][c // 2], att[1][c // 2]
        if c % 2 == 0:
            pieces.append(jnp.where(sub < 4, lo, pltpu.roll(hi, 4, 0)))
        else:
            pieces.append(jnp.where(sub < 4, pltpu.roll(lo, 4, 0), hi))
    attended = jnp.concatenate(pieces, axis=1).astype(BF16)
    values = []
    for h in range(4):
        got = dot(attended, uv[h])
        values.append(jnp.where(sub % 2 == 0, got[h : h + 1], got[4 + h : 5 + h]))
    head_values = jnp.concatenate(values, axis=1).astype(BF16)
    weights[1].wait()
    partial = dot(head_values, wo[...])
    for j in range(REDUCERS):
        attn_out[j] = packed(partial, j)

    for chip in chips:

        @pl.when(jnp.logical_and(chip < REDUCERS, k != 2 * chip))
        def _(chip=chip):
            send(attn_out.at[chip], attn_in.at[k], 2, plane + 2 * chip)

    reducer = jnp.logical_and(k % 2 == 0, k < 2 * REDUCERS)

    @pl.when(reducer)
    def _():
        j = own_chip
        attn_in[k] = attn_out[j]
        own_hid = hid_tiles[j]
        wait_for(recv_sem.at[2], attn_in, KV - 1)
        mine = (jnp.sum(attn_in[...], axis=0) + own_hid).astype(BF16).astype(F32)
        row_tiles[z] = mine
        stream_own[...] = mine
        send_row(stream_own, row_tiles.at[z], 3)
        wait_for(recv_sem.at[3], row_tiles, ROWS - 1)
        tiles = []
        for c in range(4):
            tile = None
            for zz in range(ROWS):
                shift = (2 * zz - 2 * c) % 8
                piece = row_tiles[zz]
                if shift:
                    piece = pltpu.roll(piece, shift, 0)
                tile = piece if tile is None else jnp.where(sub // 2 == zz, piece, tile)
            tiles.append(tile)
        for u in range(2):
            both = jnp.concatenate(tiles[2 * u : 2 * u + 2], axis=0).astype(BF16)
            wide[u] = both
            stream_all[j, u] = both
        send_kv(lambda peer: wide, stream_all.at[j], 4)
        wait_for(recv_sem.at[4], stream_all, REDUCERS - 1)

    @pl.when(jnp.logical_not(reducer))
    def _():
        wait_for(recv_sem.at[4], stream_all, REDUCERS)

    parts = stream_all[...].astype(F32)
    stream = jnp.concatenate(
        [parts[t // 4, (t // 2) % 2, 8 * (t % 2) : 8 * (t % 2) + 8] for t in range(D // 128)], axis=1
    )
    mean_sq = jnp.sum(stream * stream, axis=1, keepdims=True) * (1.0 / D)
    normed = (stream * lax.rsqrt(mean_sq + 1e-06) * gain[...].astype(F32).reshape(1, D)).astype(BF16)
    for copy in weights[2:4]:
        copy.wait()
    gate_proj = dot(normed, wg[...], ((1,), (1,)))
    up_proj = dot(normed, wu[...], ((1,), (1,)))
    hidden = (gate_proj / (1.0 + jnp.exp(-gate_proj)) * up_proj).astype(BF16)
    weights[4].wait()
    down = dot(hidden, wd[...])
    down = jnp.concatenate([down, jnp.zeros((8, 128), F32)], axis=1)
    for p in range(KV):
        tile, shift = divmod(OUT_COLS * p, 128)
        three = [down[:, 128 * (tile + i) : 128 * (tile + i + 1)] for i in range(3)]
        if shift:
            turned = [pltpu.roll(t, 128 - shift, 1) for t in three]
            two = [jnp.where(lane < 128 - shift, turned[i], turned[i + 1]) for i in range(2)]
        else:
            two = three[:2]
        down_out[p] = jnp.concatenate(two, axis=0).astype(BF16)
    down_in[k] = down_out[k]
    send_kv(lambda peer: down_out.at[peer], down_in.at[k], 5)

    own_tile = lax.div(7 * k, 4)
    wide_stream[:, pl.ds(0, D)] = stream
    wide_stream[:, pl.ds(D, 512)] = jnp.zeros((8, 512), F32)
    own_stream = wide_stream[:, pl.ds(pl.multiple_of(own_tile * 128, 128), 512)]
    own_stream = pltpu.roll(own_stream, lax.rem(512 - (OUT_COLS * k - 128 * own_tile), 512), 1)[:, :256]

    wait_for(recv_sem.at[5], down_in, KV - 1)
    mine = jnp.sum(down_in[...].astype(F32), axis=0)
    last_own[...] = mine
    last_in[z] = mine
    send_row(last_own, last_in.at[z], 6)
    wait_for(recv_sem.at[6], last_in, ROWS - 1)
    final = jnp.sum(last_in[...], axis=0)
    result = jnp.concatenate([final[0:8], final[8:16]], axis=1) + own_stream
    own = result[0:2]
    for zz in range(1, ROWS):
        own = jnp.where(z == zz, result[2 * zz : 2 * zz + 2], own)
    out_ref[...] = own[:, :OUT_COLS]

    for i, buffer in ((1, part_in), (5, down_in)):
        wait_for(send_sem.at[i], buffer, KV - 1)
    wait_for(send_sem.at[6], last_in, ROWS - 1)

    @pl.when(reducer)
    def _():
        wait_for(send_sem.at[2], attn_out, REDUCERS - 1)
        wait_for(send_sem.at[3], row_tiles, ROWS - 1)
        sent = s.at[0, pl.ds(0, 16), pl.ds(0, 128 * (KV - 1))]
        pltpu.make_async_copy(sent, sent, send_sem.at[4]).wait()

    @pl.when(jnp.logical_not(reducer))
    def _():
        wait_for(send_sem.at[2], attn_out, REDUCERS)


def body(query, latent_cache, new_latent, lengths, w_uv, w_o, hidden_in, norm_gain, w_gate, w_up, w_down):
    anywhere = pl.BlockSpec(memory_space=pl.ANY)
    vmem = pltpu.VMEM
    return pl.pallas_call(
        kernel,
        out_shape=jax.ShapeDtypeStruct((HERE, OUT_COLS), F32),
        in_specs=[anywhere] * 3 + [pl.BlockSpec(memory_space=pltpu.SMEM)] + [anywhere] * 7,
        out_specs=pl.BlockSpec(memory_space=vmem),
        scratch_shapes=[
            vmem((HERE, QK, HEADS), BF16),
            vmem((HERE, QK, SPAN), BF16),
            vmem((HERE, QK), BF16),
            vmem((4, LATENT, HEAD_DIM), BF16),
            vmem((4 * HEAD_DIM, D), BF16),
            vmem((HERE, D), BF16),
            vmem((D,), BF16),
            vmem((LOCAL_FF, D), BF16),
            vmem((LOCAL_FF, D), BF16),
            vmem((LOCAL_FF, D), BF16),
            vmem((HERE, HEADS, QK), BF16),
            vmem((HERE, HEADS, SPAN), F32),
            vmem((HERE, HEADS, SPAN), BF16),
            vmem((HERE, HEADS, LATENT), F32),
            vmem((REDUCERS, 8, 128), F32),
            vmem((KV // 2, 2, HERE + 1, 16, 128), BF16),
            vmem((KV, HERE + 1, 16, 128), BF16),
            vmem((REDUCERS, 8, 128), F32),
            vmem((KV, 8, 128), F32),
            vmem((ROWS, 8, 128), F32),
            vmem((8, 128), F32),
            vmem((REDUCERS, 2, 16, 128), BF16),
            vmem((2, 16, 128), BF16),
            vmem((KV, 16, 128), BF16),
            vmem((KV, 16, 128), BF16),
            vmem((16, 128), F32),
            vmem((ROWS, 16, 128), F32),
            vmem((8, D + 512), F32),
            pltpu.SemaphoreType.DMA((9,)),
            pltpu.SemaphoreType.DMA((HERE, CHUNKS)),
            pltpu.SemaphoreType.DMA((7,)),
            pltpu.SemaphoreType.DMA((7,)),
        ],
        compiler_params=pltpu.CompilerParams(
            collective_id=0, has_side_effects=True, vmem_limit_bytes=60 * 1024 * 1024
        ),
    )(
        jnp.swapaxes(query, 1, 2),
        jnp.swapaxes(latent_cache, 1, 2),
        new_latent,
        lengths,
        w_uv,
        w_o,
        hidden_in,
        norm_gain,
        w_gate.T,
        w_up.T,
        w_down,
    )


def solution(mesh):
    placed = (
        P("row", None, None),
        P("row", "kv", None),
        P("row", None),
        P("row"),
        P("kv", None, None),
        P("kv", None),
        P("row", None),
        P(),
        P(None, ("row", "kv")),
        P(None, ("row", "kv")),
        P(("row", "kv"), None),
    )
    return jax.shard_map(body, mesh=mesh, in_specs=placed, out_specs=P("row", "kv"), check_vma=False)
```

```python
import jax
import jax.numpy as jnp
from jax import lax
from jax.experimental import pallas as pl
from jax.experimental.pallas import tpu as pltpu
from jax.sharding import PartitionSpec as P

LOGICAL = pl.DeviceIdType.LOGICAL
F32, BF16 = jnp.float32, jnp.bfloat16

HEADS, LATENT, ROPE, HEAD_DIM, QK = 128, 512, 64, 128, 576
D, LOCAL_FF, SPAN = 7168, 144, 5120
KV, ROWS, HERE = 32, 4, 2
OUT_COLS = D // KV
CHUNK = 1024
BLOCK = 256
CHUNKS = SPAN // CHUNK
REDUCERS = 14
LOG2E = 1.4426950408889634
SCALE2 = LOG2E * (HEAD_DIM + ROPE) ** -0.5
NEG_FILL = -1e30


def dot(a, b, dims=((1,), (0,))):
    return lax.dot_general(a, b, (dims, ((), ())), preferred_element_type=F32)


def kernel(
    q_hbm, cache_hbm, new_hbm, lengths_ref, uv_hbm, wo_hbm, hid_hbm, gain_hbm, gate_hbm, up_hbm, down_hbm,
    out_ref,
    qt, kt, new, uv, wo, hid_in, gain, wg, wu, wd,
    q, s, w, acc, hid_tiles,
    part_out, part_in, attn_out, attn_in, row_tiles, stream_own, stream_all, wide,
    down_out, down_in, last_own, last_in, wide_stream,
    in_sem, cache_sem, send_sem, recv_sem,
):
    k = lax.axis_index("kv")
    z = lax.axis_index("row")

    small = [
        pltpu.make_async_copy(src, dst, in_sem.at[i])
        for i, (src, dst) in enumerate(((q_hbm, qt), (new_hbm, new), (hid_hbm, hid_in), (gain_hbm, gain)))
    ]
    for copy in small:
        copy.start()
    cache = [
        [
            pltpu.make_async_copy(
                cache_hbm.at[r, :, pl.ds(c * CHUNK, CHUNK)], kt.at[r, :, pl.ds(c * CHUNK, CHUNK)], cache_sem.at[r, c]
            )
            for c in range(CHUNKS)
        ]
        for r in range(HERE)
    ]
    for r in range(HERE):
        for c in range(CHUNKS):
            cache[r][c].start()
    weights = [
        pltpu.make_async_copy(src, dst, in_sem.at[4 + i])
        for i, (src, dst) in enumerate(((uv_hbm, uv), (wo_hbm, wo), (gate_hbm, wg), (up_hbm, wu), (down_hbm, wd)))
    ]

    barrier = pltpu.get_barrier_semaphore()

    plane = z * KV
    own_chip, own_core = lax.div(k, 2), lax.rem(k, 2)
    xs = [4 * lax.rem(lax.div(own_chip, 4) + d, 4) for d in range(4)]
    ys = [lax.rem(lax.rem(own_chip, 4) + d, 4) for d in range(4)]
    cores = [own_core, 1 - own_core]
    offsets = sorted(((dx, dy) for dx in range(4) for dy in range(4)), key=lambda o: -min(o[0], 4 - o[0]) - min(o[1], 4 - o[1]))
    chips = [xs[dx] + ys[dy] for dx, dy in offsets]
    peers = [2 * chip + core for chip in chips for core in cores]
    del peers[-2]
    zs = [KV * lax.rem(z + d, ROWS) for d in range(ROWS)]
    row_peers = [zs[d] + k for d in (2, 1, 3)]
    near = [(lax.div(xs[dx], 4) * 2 + core, plane + 2 * (xs[dx] + ys[0]) + core) for dx in (2, 1, 3, 0) for core in cores]
    del near[-2]
    far = sorted(((dz, dy) for dz in range(ROWS) for dy in range(4)), key=lambda o: -min(o[0], 4 - o[0]) - min(o[1], 4 - o[1]))
    far = [(ys[dy], zs[dz] + 2 * (xs[0] + ys[dy]) + own_core, dz, dy) for dz, dy in far[:-1]]
    for peer in [plane + p for p in peers] + [device for _, device, dz, _ in far if dz]:
        pl.semaphore_signal(barrier, inc=1, device_id=peer, device_id_type=LOGICAL)

    def send(src, dst, lane, device):
        pltpu.make_async_remote_copy(
            src_ref=src, dst_ref=dst, send_sem=send_sem.at[lane], recv_sem=recv_sem.at[lane],
            device_id=device, device_id_type=LOGICAL,
        ).start()

    def send_kv(src, dst, lane):
        for peer in peers:
            send(src(peer), dst, lane, plane + peer)

    def send_row(src, dst, lane):
        for peer in row_peers:
            send(src, dst, lane, peer)

    def wait_for(sem, buffer, count):
        span = buffer.at[pl.ds(0, count)]
        pltpu.make_async_copy(span, span, sem).wait()

    sub = lax.broadcasted_iota(jnp.int32, (8, 128), 0)
    lane = lax.broadcasted_iota(jnp.int32, (8, 128), 1)

    small[0].wait()
    for r in range(HERE):
        q[r] = qt[r].astype(F32).T.astype(BF16)

    def packed(rows, j):
        base = 512 * j
        tile = rows[:, base : base + 128]
        for c in range(1, 4):
            tile = jnp.where(sub // 2 == c, rows[:, base + 128 * c : base + 128 * (c + 1)], tile)
        return tile

    position = lax.broadcasted_iota(jnp.int32, (1, BLOCK), 1) + k * SPAN

    def scores(r, c):
        cache[r][c].wait()
        most = None
        for first in range(c * CHUNK, (c + 1) * CHUNK, BLOCK):
            cols = pl.ds(first, BLOCK)
            raw = dot(q[r], kt[r, :, cols]) * SCALE2
            raw = jnp.where(position + first < lengths_ref[r], raw, NEG_FILL)
            s[r, :, cols] = raw
            for part in range(0, BLOCK, 128):
                piece = raw[:, part : part + 128]
                most = piece if most is None else jnp.maximum(most, piece)
        return most

    def weigh(r, c, top):
        cols = pl.ds(c * CHUNK, CHUNK)
        value = jnp.exp2(s[r, :, cols] - top)
        w[r, :, cols] = value.astype(BF16)
        added = value[:, :128]
        for part in range(128, CHUNK, 128):
            added = added + value[:, part : part + 128]
        return added

    def highest(r, parts):
        most = parts[0]
        for part in parts[1:]:
            most = jnp.maximum(most, part)
        new_score = jnp.sum(q[r].astype(F32) * new[r : r + 1, :].astype(F32), axis=1, keepdims=True) * SCALE2
        return new_score, jnp.maximum(jnp.max(most, axis=1, keepdims=True), new_score)

    def summed(parts):
        added = parts[0]
        for part in parts[1:]:
            added = added + part
        return jnp.sum(added, axis=1, keepdims=True)

    parts = [scores(0, c) for c in range(CHUNKS)]
    small[1].wait()
    new0, top0 = highest(0, parts)
    weights[0].start()
    weights[1].start()
    parts, sums = [], []
    for c in range(CHUNKS):
        parts.append(scores(1, c))
        sums.append(weigh(0, c, top0))
    for copy in weights[2:]:
        copy.start()
    new1, top1 = highest(1, parts)
    new_score, top = [new0, new1], [top0, top1]
    total = [summed(sums), summed([weigh(1, c, top1) for c in range(CHUNKS)])]
    for r in range(HERE):
        acc[r] = dot(w[r], kt[r, :LATENT, :], ((1,), (1,)))

    half = lax.broadcasted_iota(jnp.int32, (16, 8, 128), 1) < 4
    left = lax.broadcasted_iota(jnp.int32, (HEADS, 128), 1) < 64
    wide_zero = jnp.zeros((HEADS, 128), F32)

    def share(first, second):
        t0, t1 = first.reshape(16, 8, 128), second.reshape(16, 8, 128)
        return jnp.where(half, t0, pltpu.roll(t1, 4, 1)), jnp.where(half, pltpu.roll(t0, 4, 1), t1)

    def rounded(value):
        return value.astype(BF16).astype(F32)

    logs = []
    for r in range(HERE):
        own_new = jnp.where(k == 0, jnp.exp2(new_score[r] - top[r]), 0.0)
        norm = jnp.maximum(total[r] + own_new, 1e-30)
        log_total = top[r] + jnp.log(norm) * LOG2E
        high = rounded(log_total)
        middle = rounded(log_total - high)
        low = log_total - high - middle
        logs.append(share(jnp.where(left, high, middle), jnp.where(left, low, wide_zero)))
        mine = (acc[r] + own_new * new[r : r + 1, :LATENT].astype(F32)) * (1.0 / norm)
        quarters = [mine[:, 128 * c : 128 * c + 128] for c in range(4)]
        both = [share(quarters[2 * u], quarters[2 * u + 1]) for u in range(2)]
        for core in range(2):
            part_out[:, core, r] = jnp.concatenate([both[0][core], both[1][core]], axis=1).astype(BF16)
    for core in range(2):
        part_out[:, core, HERE] = jnp.concatenate([logs[0][core], logs[1][core]], axis=1).astype(BF16)
    pl.semaphore_wait(barrier, KV - 1 + 12)
    send_kv(lambda peer: part_out.at[lax.div(peer, 2), lax.rem(peer, 2)], part_in.at[k], 1)
    part_in[k] = part_out[own_chip, own_core]

    for copy in small[2:]:
        copy.wait()
    hid_f = hid_in[...].astype(F32)
    hid_rows = jnp.where(lax.broadcasted_iota(jnp.int32, (8, D), 0) % 2 == 0, hid_f[0:1], hid_f[1:2])

    for j in range(REDUCERS):
        hid_tiles[j] = packed(hid_rows, j)

    wait_for(recv_sem.at[1], part_in, KV - 1)
    weights[0].wait()
    att = []
    for r in range(HERE):
        log_parts = part_in[:, HERE, 8 * r : 8 * r + 8].astype(F32)
        log_parts = log_parts + pltpu.roll(log_parts, 64, 2)
        log_parts = log_parts + pltpu.roll(log_parts, 4, 1)
        factor = jnp.exp2(log_parts - jnp.max(log_parts, axis=0)[None])
        factor = factor * (1.0 / jnp.sum(factor, axis=0))[None]
        data = part_in[:, r].astype(F32)
        att.append([jnp.sum(data[:, 8 * u : 8 * u + 8] * factor, axis=0) for u in range(2)])
    pieces = []
    for c in range(4):
        lo, hi = att[0][c // 2], att[1][c // 2]
        if c % 2 == 0:
            pieces.append(jnp.where(sub < 4, lo, pltpu.roll(hi, 4, 0)))
        else:
            pieces.append(jnp.where(sub < 4, pltpu.roll(lo, 4, 0), hi))
    attended = jnp.concatenate(pieces, axis=1).astype(BF16)
    values = []
    for h in range(4):
        got = dot(attended, uv[h])
        values.append(jnp.where(sub % 2 == 0, got[h : h + 1], got[4 + h : 5 + h]))
    head_values = jnp.concatenate(values, axis=1).astype(BF16)
    weights[1].wait()
    partial = dot(head_values, wo[...])
    for j in range(REDUCERS):
        attn_out[j] = packed(partial, j)

    for chip in chips:

        @pl.when(jnp.logical_and(chip < REDUCERS, k != 2 * chip))
        def _(chip=chip):
            send(attn_out.at[chip], attn_in.at[k], 2, plane + 2 * chip)

    reducer = jnp.logical_and(k % 2 == 0, k < 2 * REDUCERS)

    @pl.when(reducer)
    def _():
        j = own_chip
        attn_in[k] = attn_out[j]
        own_hid = hid_tiles[j]
        wait_for(recv_sem.at[2], attn_in, KV - 1)
        mine = (jnp.sum(attn_in[...], axis=0) + own_hid).astype(BF16).astype(F32)
        row_tiles[z] = mine
        stream_own[...] = mine
        send_row(stream_own, row_tiles.at[z], 3)
        wait_for(recv_sem.at[3], row_tiles, ROWS - 1)
        tiles = []
        for c in range(4):
            tile = None
            for zz in range(ROWS):
                shift = (2 * zz - 2 * c) % 8
                piece = row_tiles[zz]
                if shift:
                    piece = pltpu.roll(piece, shift, 0)
                tile = piece if tile is None else jnp.where(sub // 2 == zz, piece, tile)
            tiles.append(tile)
        for u in range(2):
            both = jnp.concatenate(tiles[2 * u : 2 * u + 2], axis=0).astype(BF16)
            wide[u] = both
            stream_all[j, u] = both
        send_kv(lambda peer: wide, stream_all.at[j], 4)
        wait_for(recv_sem.at[4], stream_all, REDUCERS - 1)

    @pl.when(jnp.logical_not(reducer))
    def _():
        wait_for(recv_sem.at[4], stream_all, REDUCERS)

    parts = stream_all[...].astype(F32)
    stream = jnp.concatenate(
        [parts[t // 4, (t // 2) % 2, 8 * (t % 2) : 8 * (t % 2) + 8] for t in range(D // 128)], axis=1
    )
    scaled = (stream * gain[...].astype(F32).reshape(1, D)).astype(BF16)
    for copy in weights[2:4]:
        copy.wait()

    def project(weight):
        parts = [
            dot(scaled[:, first : first + 3584], weight[:, first : first + 3584], ((1,), (1,))) for first in (0, 3584)
        ]
        return parts[0] + parts[1]

    gate_proj, up_proj = project(wg), project(wu)
    rstd = lax.rsqrt(jnp.sum(stream * stream, axis=1, keepdims=True) * (1.0 / D) + 1e-06)
    gate_proj = gate_proj * rstd
    hidden = (gate_proj / (1.0 + jnp.exp(-gate_proj)) * (up_proj * rstd)).astype(BF16)
    weights[4].wait()
    down = dot(hidden, wd[...])
    down = jnp.concatenate([down, jnp.zeros((8, 128), F32)], axis=1)
    for p in range(KV):
        tile, shift = divmod(OUT_COLS * p, 128)
        three = [down[:, 128 * (tile + i) : 128 * (tile + i + 1)] for i in range(3)]
        if shift:
            turned = [pltpu.roll(t, 128 - shift, 1) for t in three]
            two = [jnp.where(lane < 128 - shift, turned[i], turned[i + 1]) for i in range(2)]
        else:
            two = three[:2]
        down_out[p // 8 * 2 + p % 2, p // 2 % 4] = jnp.concatenate(two, axis=0).astype(BF16)
    own_near = lax.div(xs[0], 4) * 2 + own_core
    for block, device in near:
        send(down_out.at[block], down_in.at[own_near], 5, device)
    down_in[own_near] = down_out[own_near]

    own_tile = lax.div(7 * k, 4)
    wide_stream[:, pl.ds(0, D)] = stream
    wide_stream[:, pl.ds(D, 512)] = jnp.zeros((8, 512), F32)
    own_stream = wide_stream[:, pl.ds(pl.multiple_of(own_tile * 128, 128), 512)]
    own_stream = pltpu.roll(own_stream, lax.rem(512 - (OUT_COLS * k - 128 * own_tile), 512), 1)[:, :256]

    wait_for(recv_sem.at[5], down_in, 7)
    last_own[...] = jnp.sum(down_in[...].astype(F32), axis=0).astype(BF16)
    own_far = 4 * z + ys[0]
    for y, device, _, _ in far:
        send(last_own.at[y], last_in.at[own_far], 6, device)
    last_in[own_far] = last_own[ys[0]]
    wait_for(recv_sem.at[6], last_in, 15)
    final = jnp.sum(last_in[...].astype(F32), axis=0)
    result = jnp.concatenate([final[0:8], final[8:16]], axis=1) + own_stream
    own = result[0:2]
    for zz in range(1, ROWS):
        own = jnp.where(z == zz, result[2 * zz : 2 * zz + 2], own)
    out_ref[...] = own[:, :OUT_COLS]

    for i, buffer, count in ((1, part_in, KV - 1), (5, down_in, 7), (6, last_in, 15)):
        wait_for(send_sem.at[i], buffer, count)

    @pl.when(reducer)
    def _():
        wait_for(send_sem.at[2], attn_out, REDUCERS - 1)
        wait_for(send_sem.at[3], row_tiles, ROWS - 1)
        sent = s.at[0, pl.ds(0, 16), pl.ds(0, 128 * (KV - 1))]
        pltpu.make_async_copy(sent, sent, send_sem.at[4]).wait()

    @pl.when(jnp.logical_not(reducer))
    def _():
        wait_for(send_sem.at[2], attn_out, REDUCERS)


def body(query, latent_cache, new_latent, lengths, w_uv, w_o, hidden_in, norm_gain, w_gate, w_up, w_down):
    anywhere = pl.BlockSpec(memory_space=pl.ANY)
    vmem = pltpu.VMEM
    return pl.pallas_call(
        kernel,
        out_shape=jax.ShapeDtypeStruct((HERE, OUT_COLS), F32),
        in_specs=[anywhere] * 3 + [pl.BlockSpec(memory_space=pltpu.SMEM)] + [anywhere] * 7,
        out_specs=pl.BlockSpec(memory_space=vmem),
        scratch_shapes=[
            vmem((HERE, QK, HEADS), BF16),
            vmem((HERE, QK, SPAN), BF16),
            vmem((HERE, QK), BF16),
            vmem((4, LATENT, HEAD_DIM), BF16),
            vmem((4 * HEAD_DIM, D), BF16),
            vmem((HERE, D), BF16),
            vmem((D,), BF16),
            vmem((LOCAL_FF, D), BF16),
            vmem((LOCAL_FF, D), BF16),
            vmem((LOCAL_FF, D), BF16),
            vmem((HERE, HEADS, QK), BF16),
            vmem((HERE, HEADS, SPAN), F32),
            vmem((HERE, HEADS, SPAN), BF16),
            vmem((HERE, HEADS, LATENT), F32),
            vmem((REDUCERS, 8, 128), F32),
            vmem((KV // 2, 2, HERE + 1, 16, 128), BF16),
            vmem((KV, HERE + 1, 16, 128), BF16),
            vmem((REDUCERS, 8, 128), F32),
            vmem((KV, 8, 128), F32),
            vmem((ROWS, 8, 128), F32),
            vmem((8, 128), F32),
            vmem((REDUCERS, 2, 16, 128), BF16),
            vmem((2, 16, 128), BF16),
            vmem((8, 4, 16, 128), BF16),
            vmem((8, 4, 16, 128), BF16),
            vmem((4, 16, 128), BF16),
            vmem((16, 16, 128), BF16),
            vmem((8, D + 512), F32),
            pltpu.SemaphoreType.DMA((9,)),
            pltpu.SemaphoreType.DMA((HERE, CHUNKS)),
            pltpu.SemaphoreType.DMA((7,)),
            pltpu.SemaphoreType.DMA((7,)),
        ],
        compiler_params=pltpu.CompilerParams(
            collective_id=0, has_side_effects=True, vmem_limit_bytes=60 * 1024 * 1024
        ),
    )(
        jnp.swapaxes(query, 1, 2),
        jnp.swapaxes(latent_cache, 1, 2),
        new_latent,
        lengths,
        w_uv,
        w_o,
        hidden_in,
        norm_gain,
        w_gate.T,
        w_up.T,
        w_down,
    )


def solution(mesh):
    placed = (
        P("row", None, None),
        P("row", "kv", None),
        P("row", None),
        P("row"),
        P("kv", None, None),
        P("kv", None),
        P("row", None),
        P(),
        P(None, ("row", "kv")),
        P(None, ("row", "kv")),
        P(("row", "kv"), None),
    )
    return jax.shard_map(body, mesh=mesh, in_specs=placed, out_specs=P("row", "kv"), check_vma=False)
```

```python
import jax
import jax.numpy as jnp
from jax import lax
from jax.experimental import pallas as pl
from jax.experimental.pallas import tpu as pltpu
from jax.sharding import PartitionSpec as P

LOGICAL = pl.DeviceIdType.LOGICAL
F32, BF16 = jnp.float32, jnp.bfloat16

HEADS, LATENT, ROPE, HEAD_DIM, QK = 128, 512, 64, 128, 576
D, LOCAL_FF, SPAN = 7168, 144, 5120
KV, ROWS, HERE = 32, 4, 2
OUT_COLS = D // KV
CHUNK = 1024
BLOCK = 256
CHUNKS = SPAN // CHUNK
REDUCERS = 14
LOG2E = 1.4426950408889634
SCALE2 = LOG2E * (HEAD_DIM + ROPE) ** -0.5
NEG_FILL = -1e30


def dot(a, b, dims=((1,), (0,))):
    return lax.dot_general(a, b, (dims, ((), ())), preferred_element_type=F32)


def kernel(
    q_hbm, cache_hbm, new_hbm, lengths_ref, uv_hbm, wo_hbm, hid_hbm, gain_hbm, gate_hbm, up_hbm, down_hbm,
    out_ref,
    qt, kt, new, uv, wo, hid_in, gain, wg, wu, wd,
    q, s, w, acc, hid_tiles,
    part_out, part_in, attn_out, attn_in, row_tiles, stream_own, stream_all, wide,
    down_out, down_in, last_own, last_in, wide_stream,
    in_sem, cache_sem, send_sem, recv_sem,
):
    k = lax.axis_index("kv")
    z = lax.axis_index("row")

    small = [
        pltpu.make_async_copy(src, dst, in_sem.at[i])
        for i, (src, dst) in enumerate(((q_hbm, qt), (new_hbm, new), (hid_hbm, hid_in), (gain_hbm, gain)))
    ]
    for copy in small:
        copy.start()
    cache = [
        [
            pltpu.make_async_copy(
                cache_hbm.at[r, :, pl.ds(c * CHUNK, CHUNK)], kt.at[r, :, pl.ds(c * CHUNK, CHUNK)], cache_sem.at[r, c]
            )
            for c in range(CHUNKS)
        ]
        for r in range(HERE)
    ]
    for r in range(HERE):
        for c in range(CHUNKS):
            cache[r][c].start()
    weights = [
        pltpu.make_async_copy(src, dst, in_sem.at[4 + i])
        for i, (src, dst) in enumerate(((uv_hbm, uv), (wo_hbm, wo), (gate_hbm, wg), (up_hbm, wu), (down_hbm, wd)))
    ]

    barrier = pltpu.get_barrier_semaphore()

    plane = z * KV
    own_chip, own_core = lax.div(k, 2), lax.rem(k, 2)
    xs = [4 * lax.rem(lax.div(own_chip, 4) + d, 4) for d in range(4)]
    ys = [lax.rem(lax.rem(own_chip, 4) + d, 4) for d in range(4)]
    cores = [own_core, 1 - own_core]
    offsets = sorted(((dx, dy) for dx in range(4) for dy in range(4)), key=lambda o: -min(o[0], 4 - o[0]) - min(o[1], 4 - o[1]))
    chips = [xs[dx] + ys[dy] for dx, dy in offsets]
    peers = [2 * chip + core for chip in chips for core in cores]
    del peers[-2]
    row_peers = [lax.rem(z + d, ROWS) * KV + k for d in (2, 1, 3)]
    for peer in [plane + p for p in peers] + row_peers:
        pl.semaphore_signal(barrier, inc=1, device_id=peer, device_id_type=LOGICAL)

    def send(src, dst, lane, device):
        pltpu.make_async_remote_copy(
            src_ref=src, dst_ref=dst, send_sem=send_sem.at[lane], recv_sem=recv_sem.at[lane],
            device_id=device, device_id_type=LOGICAL,
        ).start()

    def send_kv(src, dst, lane):
        for peer in peers:
            send(src(peer), dst, lane, plane + peer)

    def send_row(src, dst, lane):
        for peer in row_peers:
            send(src, dst, lane, peer)

    def wait_for(sem, buffer, count):
        span = buffer.at[pl.ds(0, count)]
        pltpu.make_async_copy(span, span, sem).wait()

    sub = lax.broadcasted_iota(jnp.int32, (8, 128), 0)
    lane = lax.broadcasted_iota(jnp.int32, (8, 128), 1)

    small[0].wait()
    for r in range(HERE):
        q[r] = qt[r].astype(F32).T.astype(BF16)

    def packed(rows, j):
        base = 512 * j
        tile = rows[:, base : base + 128]
        for c in range(1, 4):
            tile = jnp.where(sub // 2 == c, rows[:, base + 128 * c : base + 128 * (c + 1)], tile)
        return tile

    position = lax.broadcasted_iota(jnp.int32, (1, BLOCK), 1) + k * SPAN

    def scores(r, c):
        cache[r][c].wait()
        most = None
        for first in range(c * CHUNK, (c + 1) * CHUNK, BLOCK):
            cols = pl.ds(first, BLOCK)
            raw = dot(q[r], kt[r, :, cols]) * SCALE2
            raw = jnp.where(position + first < lengths_ref[r], raw, NEG_FILL)
            s[r, :, cols] = raw
            for part in range(0, BLOCK, 128):
                piece = raw[:, part : part + 128]
                most = piece if most is None else jnp.maximum(most, piece)
        return most

    def weigh(r, c, top):
        cols = pl.ds(c * CHUNK, CHUNK)
        value = jnp.exp2(s[r, :, cols] - top)
        w[r, :, cols] = value.astype(BF16)
        added = value[:, :128]
        for part in range(128, CHUNK, 128):
            added = added + value[:, part : part + 128]
        return added

    def highest(r, parts):
        most = parts[0]
        for part in parts[1:]:
            most = jnp.maximum(most, part)
        new_score = jnp.sum(q[r].astype(F32) * new[r : r + 1, :].astype(F32), axis=1, keepdims=True) * SCALE2
        return new_score, jnp.maximum(jnp.max(most, axis=1, keepdims=True), new_score)

    def summed(parts):
        added = parts[0]
        for part in parts[1:]:
            added = added + part
        return jnp.sum(added, axis=1, keepdims=True)

    parts = [scores(0, c) for c in range(CHUNKS)]
    small[1].wait()
    new0, top0 = highest(0, parts)
    weights[0].start()
    weights[1].start()
    parts, sums = [], []
    for c in range(CHUNKS):
        parts.append(scores(1, c))
        sums.append(weigh(0, c, top0))
    for copy in weights[2:]:
        copy.start()
    new1, top1 = highest(1, parts)
    new_score, top = [new0, new1], [top0, top1]
    total = [summed(sums), summed([weigh(1, c, top1) for c in range(CHUNKS)])]
    for r in range(HERE):
        acc[r] = dot(kt[r, :LATENT, :], w[r], ((1,), (1,)))

    half = lax.broadcasted_iota(jnp.int32, (16, 8, 128), 1) < 4
    left = lax.broadcasted_iota(jnp.int32, (HEADS, 128), 1) < 64
    wide_zero = jnp.zeros((HEADS, 128), F32)

    def share(first, second):
        t0, t1 = first.reshape(16, 8, 128), second.reshape(16, 8, 128)
        return jnp.where(half, t0, pltpu.roll(t1, 4, 1)), jnp.where(half, pltpu.roll(t0, 4, 1), t1)

    def rounded(value):
        return value.astype(BF16).astype(F32)

    logs = []
    for r in range(HERE):
        own_new = jnp.where(k == 0, jnp.exp2(new_score[r] - top[r]), 0.0)
        norm = jnp.maximum(total[r] + own_new, 1e-30)
        log_total = top[r] + jnp.log(norm) * LOG2E
        high = rounded(log_total)
        middle = rounded(log_total - high)
        low = log_total - high - middle
        logs.append(share(jnp.where(left, high, middle), jnp.where(left, low, wide_zero)))
        mine = (acc[r].T + own_new * new[r : r + 1, :LATENT].astype(F32)) * (1.0 / norm)
        quarters = [mine[:, 128 * c : 128 * c + 128] for c in range(4)]
        both = [share(quarters[2 * u], quarters[2 * u + 1]) for u in range(2)]
        for core in range(2):
            part_out[:, core, r] = jnp.concatenate([both[0][core], both[1][core]], axis=1).astype(BF16)
    for core in range(2):
        part_out[:, core, HERE] = jnp.concatenate([logs[0][core], logs[1][core]], axis=1).astype(BF16)
    pl.semaphore_wait(barrier, KV - 1 + ROWS - 1)
    send_kv(lambda peer: part_out.at[lax.div(peer, 2), lax.rem(peer, 2)], part_in.at[k], 1)
    part_in[k] = part_out[own_chip, own_core]

    for copy in small[2:]:
        copy.wait()
    hid_f = hid_in[...].astype(F32)
    hid_rows = jnp.where(lax.broadcasted_iota(jnp.int32, (8, D), 0) % 2 == 0, hid_f[0:1], hid_f[1:2])

    for j in range(REDUCERS):
        hid_tiles[j] = packed(hid_rows, j)

    wait_for(recv_sem.at[1], part_in, KV - 1)
    weights[0].wait()
    att = []
    for r in range(HERE):
        log_parts = part_in[:, HERE, 8 * r : 8 * r + 8].astype(F32)
        log_parts = log_parts + pltpu.roll(log_parts, 64, 2)
        log_parts = log_parts + pltpu.roll(log_parts, 4, 1)
        factor = jnp.exp2(log_parts - jnp.max(log_parts, axis=0)[None])
        factor = factor * (1.0 / jnp.sum(factor, axis=0))[None]
        data = part_in[:, r].astype(F32)
        att.append([jnp.sum(data[:, 8 * u : 8 * u + 8] * factor, axis=0) for u in range(2)])
    pieces = []
    for c in range(4):
        lo, hi = att[0][c // 2], att[1][c // 2]
        if c % 2 == 0:
            pieces.append(jnp.where(sub < 4, lo, pltpu.roll(hi, 4, 0)))
        else:
            pieces.append(jnp.where(sub < 4, pltpu.roll(lo, 4, 0), hi))
    attended = jnp.concatenate(pieces, axis=1).astype(BF16)
    values = []
    for h in range(4):
        got = dot(attended, uv[h])
        values.append(jnp.where(sub % 2 == 0, got[h : h + 1], got[4 + h : 5 + h]))
    head_values = jnp.concatenate(values, axis=1).astype(BF16)
    weights[1].wait()
    partial = dot(head_values, wo[...])
    for j in range(REDUCERS):
        attn_out[j] = packed(partial, j)

    for chip in chips:

        @pl.when(jnp.logical_and(chip < REDUCERS, k != 2 * chip))
        def _(chip=chip):
            send(attn_out.at[chip], attn_in.at[k], 2, plane + 2 * chip)

    reducer = jnp.logical_and(k % 2 == 0, k < 2 * REDUCERS)

    @pl.when(reducer)
    def _():
        j = own_chip
        attn_in[k] = attn_out[j]
        own_hid = hid_tiles[j]
        wait_for(recv_sem.at[2], attn_in, KV - 1)
        mine = (jnp.sum(attn_in[...], axis=0) + own_hid).astype(BF16).astype(F32)
        row_tiles[z] = mine
        stream_own[...] = mine
        send_row(stream_own, row_tiles.at[z], 3)
        wait_for(recv_sem.at[3], row_tiles, ROWS - 1)
        tiles = []
        for c in range(4):
            tile = None
            for zz in range(ROWS):
                shift = (2 * zz - 2 * c) % 8
                piece = row_tiles[zz]
                if shift:
                    piece = pltpu.roll(piece, shift, 0)
                tile = piece if tile is None else jnp.where(sub // 2 == zz, piece, tile)
            tiles.append(tile)
        for u in range(2):
            both = jnp.concatenate(tiles[2 * u : 2 * u + 2], axis=0).astype(BF16)
            wide[u] = both
            stream_all[j, u] = both
        send_kv(lambda peer: wide, stream_all.at[j], 4)
        wait_for(recv_sem.at[4], stream_all, REDUCERS - 1)

    @pl.when(jnp.logical_not(reducer))
    def _():
        wait_for(recv_sem.at[4], stream_all, REDUCERS)

    parts = stream_all[...].astype(F32)
    stream = jnp.concatenate(
        [parts[t // 4, (t // 2) % 2, 8 * (t % 2) : 8 * (t % 2) + 8] for t in range(D // 128)], axis=1
    )
    mean_sq = jnp.sum(stream * stream, axis=1, keepdims=True) * (1.0 / D)
    normed = (stream * lax.rsqrt(mean_sq + 1e-06) * gain[...].astype(F32).reshape(1, D)).astype(BF16)
    for copy in weights[2:4]:
        copy.wait()
    gate_proj = dot(normed, wg[...], ((1,), (1,)))
    up_proj = dot(normed, wu[...], ((1,), (1,)))
    hidden = (gate_proj / (1.0 + jnp.exp(-gate_proj)) * up_proj).astype(BF16)
    weights[4].wait()
    down = dot(hidden, wd[...])
    down = jnp.concatenate([down, jnp.zeros((8, 128), F32)], axis=1)
    for p in range(KV):
        tile, shift = divmod(OUT_COLS * p, 128)
        three = [down[:, 128 * (tile + i) : 128 * (tile + i + 1)] for i in range(3)]
        if shift:
            turned = [pltpu.roll(t, 128 - shift, 1) for t in three]
            two = [jnp.where(lane < 128 - shift, turned[i], turned[i + 1]) for i in range(2)]
        else:
            two = three[:2]
        down_out[p] = jnp.concatenate(two, axis=0).astype(BF16)
    down_in[k] = down_out[k]
    send_kv(lambda peer: down_out.at[peer], down_in.at[k], 5)

    own_tile = lax.div(7 * k, 4)
    wide_stream[:, pl.ds(0, D)] = stream
    wide_stream[:, pl.ds(D, 512)] = jnp.zeros((8, 512), F32)
    own_stream = wide_stream[:, pl.ds(pl.multiple_of(own_tile * 128, 128), 512)]
    own_stream = pltpu.roll(own_stream, lax.rem(512 - (OUT_COLS * k - 128 * own_tile), 512), 1)[:, :256]

    wait_for(recv_sem.at[5], down_in, KV - 1)
    mine = jnp.sum(down_in[...].astype(F32), axis=0)
    last_own[...] = mine
    last_in[z] = mine
    send_row(last_own, last_in.at[z], 6)
    wait_for(recv_sem.at[6], last_in, ROWS - 1)
    final = jnp.sum(last_in[...], axis=0)
    result = jnp.concatenate([final[0:8], final[8:16]], axis=1) + own_stream
    own = result[0:2]
    for zz in range(1, ROWS):
        own = jnp.where(z == zz, result[2 * zz : 2 * zz + 2], own)
    out_ref[...] = own[:, :OUT_COLS]

    for i, buffer in ((1, part_in), (5, down_in)):
        wait_for(send_sem.at[i], buffer, KV - 1)
    wait_for(send_sem.at[6], last_in, ROWS - 1)

    @pl.when(reducer)
    def _():
        wait_for(send_sem.at[2], attn_out, REDUCERS - 1)
        wait_for(send_sem.at[3], row_tiles, ROWS - 1)
        sent = s.at[0, pl.ds(0, 16), pl.ds(0, 128 * (KV - 1))]
        pltpu.make_async_copy(sent, sent, send_sem.at[4]).wait()

    @pl.when(jnp.logical_not(reducer))
    def _():
        wait_for(send_sem.at[2], attn_out, REDUCERS)


def body(query, latent_cache, new_latent, lengths, w_uv, w_o, hidden_in, norm_gain, w_gate, w_up, w_down):
    anywhere = pl.BlockSpec(memory_space=pl.ANY)
    vmem = pltpu.VMEM
    return pl.pallas_call(
        kernel,
        out_shape=jax.ShapeDtypeStruct((HERE, OUT_COLS), F32),
        in_specs=[anywhere] * 3 + [pl.BlockSpec(memory_space=pltpu.SMEM)] + [anywhere] * 7,
        out_specs=pl.BlockSpec(memory_space=vmem),
        scratch_shapes=[
            vmem((HERE, QK, HEADS), BF16),
            vmem((HERE, QK, SPAN), BF16),
            vmem((HERE, QK), BF16),
            vmem((4, LATENT, HEAD_DIM), BF16),
            vmem((4 * HEAD_DIM, D), BF16),
            vmem((HERE, D), BF16),
            vmem((D,), BF16),
            vmem((LOCAL_FF, D), BF16),
            vmem((LOCAL_FF, D), BF16),
            vmem((LOCAL_FF, D), BF16),
            vmem((HERE, HEADS, QK), BF16),
            vmem((HERE, HEADS, SPAN), F32),
            vmem((HERE, HEADS, SPAN), BF16),
            vmem((HERE, LATENT, HEADS), F32),
            vmem((REDUCERS, 8, 128), F32),
            vmem((KV // 2, 2, HERE + 1, 16, 128), BF16),
            vmem((KV, HERE + 1, 16, 128), BF16),
            vmem((REDUCERS, 8, 128), F32),
            vmem((KV, 8, 128), F32),
            vmem((ROWS, 8, 128), F32),
            vmem((8, 128), F32),
            vmem((REDUCERS, 2, 16, 128), BF16),
            vmem((2, 16, 128), BF16),
            vmem((KV, 16, 128), BF16),
            vmem((KV, 16, 128), BF16),
            vmem((16, 128), F32),
            vmem((ROWS, 16, 128), F32),
            vmem((8, D + 512), F32),
            pltpu.SemaphoreType.DMA((9,)),
            pltpu.SemaphoreType.DMA((HERE, CHUNKS)),
            pltpu.SemaphoreType.DMA((7,)),
            pltpu.SemaphoreType.DMA((7,)),
        ],
        compiler_params=pltpu.CompilerParams(
            collective_id=0, has_side_effects=True, vmem_limit_bytes=60 * 1024 * 1024
        ),
    )(
        jnp.swapaxes(query, 1, 2),
        jnp.swapaxes(latent_cache, 1, 2),
        new_latent,
        lengths,
        w_uv,
        w_o,
        hidden_in,
        norm_gain,
        w_gate.T,
        w_up.T,
        w_down,
    )


def solution(mesh):
    placed = (
        P("row", None, None),
        P("row", "kv", None),
        P("row", None),
        P("row"),
        P("kv", None, None),
        P("kv", None),
        P("row", None),
        P(),
        P(None, ("row", "kv")),
        P(None, ("row", "kv")),
        P(("row", "kv"), None),
    )
    return jax.shard_map(body, mesh=mesh, in_specs=placed, out_specs=P("row", "kv"), check_vma=False)
```

```python
import jax
import jax.numpy as jnp
from jax import lax
from jax.experimental import pallas as pl
from jax.experimental.pallas import tpu as pltpu
from jax.sharding import PartitionSpec as P

LOGICAL = pl.DeviceIdType.LOGICAL
F32, BF16 = jnp.float32, jnp.bfloat16

HEADS, LATENT, ROPE, HEAD_DIM, QK = 128, 512, 64, 128, 576
D, LOCAL_FF, SPAN = 7168, 144, 5120
KV, ROWS, HERE = 32, 4, 2
OUT_COLS = D // KV
PIECES = ((0, 1024, 3072, SPAN), (0, 2560, SPAN))
BLOCK = 256
BLOCKS = SPAN // BLOCK
REDUCERS = 14
LOG2E = 1.4426950408889634
SCALE2 = LOG2E * (HEAD_DIM + ROPE) ** -0.5
NEG_FILL = -1e30


def dot(a, b, dims=((1,), (0,))):
    return lax.dot_general(a, b, (dims, ((), ())), preferred_element_type=F32)


def kernel(
    q_hbm, cache_hbm, new_hbm, lengths_ref, uv_hbm, wo_hbm, hid_hbm, gain_hbm, gate_hbm, up_hbm, down_hbm,
    out_ref,
    qt, kt, new, uv, wo, hid_in, gain, wg, wu, wd,
    q, s, w, acc, hid_tiles,
    part_out, part_in, attn_out, attn_in, row_tiles, stream_own, stream_all, wide,
    down_out, down_in, last_own, last_in, wide_stream,
    in_sem, cache_sem, send_sem, recv_sem,
):
    k = lax.axis_index("kv")
    z = lax.axis_index("row")

    small = [
        pltpu.make_async_copy(src, dst, in_sem.at[i])
        for i, (src, dst) in enumerate(((q_hbm, qt), (new_hbm, new), (hid_hbm, hid_in), (gain_hbm, gain)))
    ]
    for copy in small:
        copy.start()
    cache = []
    for r in range(HERE):
        for c, (first, end) in enumerate(zip(PIECES[r], PIECES[r][1:])):
            span = pl.ds(first, end - first)
            copy = pltpu.make_async_copy(cache_hbm.at[r, :, span], kt.at[r, :, span], cache_sem.at[r, c])
            copy.start()
            cache.append((r, first, copy))

    weights = [
        pltpu.make_async_copy(src, dst, in_sem.at[4 + i])
        for i, (src, dst) in enumerate(((uv_hbm, uv), (wo_hbm, wo), (gate_hbm, wg), (up_hbm, wu), (down_hbm, wd)))
    ]

    barrier = pltpu.get_barrier_semaphore()

    plane = z * KV
    own_chip, own_core = lax.div(k, 2), lax.rem(k, 2)
    xs = [4 * lax.rem(lax.div(own_chip, 4) + d, 4) for d in range(4)]
    ys = [lax.rem(lax.rem(own_chip, 4) + d, 4) for d in range(4)]
    cores = [own_core, 1 - own_core]
    offsets = sorted(((dx, dy) for dx in range(4) for dy in range(4)), key=lambda o: -min(o[0], 4 - o[0]) - min(o[1], 4 - o[1]))
    chips = [xs[dx] + ys[dy] for dx, dy in offsets]
    peers = [2 * chip + core for chip in chips for core in cores]
    del peers[-2]
    row_peers = [lax.rem(z + d, ROWS) * KV + k for d in (2, 1, 3)]
    for peer in [plane + p for p in peers] + row_peers:
        pl.semaphore_signal(barrier, inc=1, device_id=peer, device_id_type=LOGICAL)

    def send(src, dst, lane, device):
        pltpu.make_async_remote_copy(
            src_ref=src, dst_ref=dst, send_sem=send_sem.at[lane], recv_sem=recv_sem.at[lane],
            device_id=device, device_id_type=LOGICAL,
        ).start()

    def send_kv(src, dst, lane):
        for peer in peers:
            send(src(peer), dst, lane, plane + peer)

    def send_row(src, dst, lane):
        for peer in row_peers:
            send(src, dst, lane, peer)

    def wait_for(sem, buffer, count):
        span = buffer.at[pl.ds(0, count)]
        pltpu.make_async_copy(span, span, sem).wait()

    sub = lax.broadcasted_iota(jnp.int32, (8, 128), 0)
    lane = lax.broadcasted_iota(jnp.int32, (8, 128), 1)

    small[0].wait()
    for r in range(HERE):
        q[r] = qt[r].astype(F32).T.astype(BF16)

    def packed(rows, j):
        base = 512 * j
        tile = rows[:, base : base + 128]
        for c in range(1, 4):
            tile = jnp.where(sub // 2 == c, rows[:, base + 128 * c : base + 128 * (c + 1)], tile)
        return tile

    position = lax.broadcasted_iota(jnp.int32, (1, BLOCK), 1) + k * SPAN

    def largest(value, so_far):
        for part in range(0, BLOCK, 128):
            piece = value[:, part : part + 128]
            so_far = piece if so_far is None else jnp.maximum(so_far, piece)
        return so_far

    def scores(r, i, so_far):
        for row, first, copy in cache:
            if (row, first) == (r, BLOCK * i):
                copy.wait()
        cols = pl.ds(BLOCK * i, BLOCK)
        raw = dot(q[r], kt[r, :, cols]) * SCALE2
        raw = jnp.where(position + BLOCK * i < lengths_ref[r], raw, NEG_FILL)
        s[r, :, cols] = raw
        return largest(raw, so_far)

    def weigh(r, i, top, so_far):
        cols = pl.ds(BLOCK * i, BLOCK)
        value = jnp.exp2(s[r, :, cols] - top)
        w[r, :, cols] = value.astype(BF16)
        for part in range(0, BLOCK, 128):
            piece = value[:, part : part + 128]
            so_far = piece if so_far is None else so_far + piece
        return so_far

    def highest(r, most):
        new_score = jnp.sum(q[r].astype(F32) * new[r : r + 1, :].astype(F32), axis=1, keepdims=True) * SCALE2
        return new_score, jnp.maximum(jnp.max(most, axis=1, keepdims=True), new_score)

    most0 = None
    for i in range(BLOCKS):
        most0 = scores(0, i, most0)
    small[1].wait()
    new0, top0 = highest(0, most0)
    most1 = sum0 = sum1 = None
    for i in range(BLOCKS):
        most1 = scores(1, i, most1)
        sum0 = weigh(0, i, top0, sum0)
    for copy in weights:
        copy.start()
    new1, top1 = highest(1, most1)
    for half in range(2):
        rows = slice(256 * half, 256 * half + 256)
        acc[0, rows] = dot(kt[0, rows, :], w[0], ((1,), (1,)))
        for i in range(BLOCKS // 2 * half, BLOCKS // 2 * (half + 1)):
            sum1 = weigh(1, i, top1, sum1)
    acc[1] = dot(kt[1, :LATENT, :], w[1], ((1,), (1,)))
    new_score, top = [new0, new1], [top0, top1]
    total = [jnp.sum(value, axis=1, keepdims=True) for value in (sum0, sum1)]

    half = lax.broadcasted_iota(jnp.int32, (16, 8, 128), 1) < 4
    left = lax.broadcasted_iota(jnp.int32, (HEADS, 128), 1) < 64
    wide_zero = jnp.zeros((HEADS, 128), F32)

    def share(first, second):
        t0, t1 = first.reshape(16, 8, 128), second.reshape(16, 8, 128)
        return jnp.where(half, t0, pltpu.roll(t1, 4, 1)), jnp.where(half, pltpu.roll(t0, 4, 1), t1)

    def rounded(value):
        return value.astype(BF16).astype(F32)

    logs = []
    for r in range(HERE):
        own_new = jnp.where(k == 0, jnp.exp2(new_score[r] - top[r]), 0.0)
        norm = jnp.maximum(total[r] + own_new, 1e-30)
        log_total = top[r] + jnp.log(norm) * LOG2E
        high = rounded(log_total)
        middle = rounded(log_total - high)
        low = log_total - high - middle
        logs.append(share(jnp.where(left, high, middle), jnp.where(left, low, wide_zero)))
        mine = (acc[r].T + own_new * new[r : r + 1, :LATENT].astype(F32)) * (1.0 / norm)
        quarters = [mine[:, 128 * c : 128 * c + 128] for c in range(4)]
        both = [share(quarters[2 * u], quarters[2 * u + 1]) for u in range(2)]
        for core in range(2):
            part_out[:, core, r] = jnp.concatenate([both[0][core], both[1][core]], axis=1).astype(BF16)
    for core in range(2):
        part_out[:, core, HERE] = jnp.concatenate([logs[0][core], logs[1][core]], axis=1).astype(BF16)
    pl.semaphore_wait(barrier, KV - 1 + ROWS - 1)
    send_kv(lambda peer: part_out.at[lax.div(peer, 2), lax.rem(peer, 2)], part_in.at[k], 1)
    part_in[k] = part_out[own_chip, own_core]

    for copy in small[2:]:
        copy.wait()
    hid_f = hid_in[...].astype(F32)
    hid_rows = jnp.where(lax.broadcasted_iota(jnp.int32, (8, D), 0) % 2 == 0, hid_f[0:1], hid_f[1:2])

    for j in range(REDUCERS):
        hid_tiles[j] = packed(hid_rows, j)

    wait_for(recv_sem.at[1], part_in, KV - 1)
    weights[0].wait()
    att = []
    for r in range(HERE):
        log_parts = part_in[:, HERE, 8 * r : 8 * r + 8].astype(F32)
        log_parts = log_parts + pltpu.roll(log_parts, 64, 2)
        log_parts = log_parts + pltpu.roll(log_parts, 4, 1)
        factor = jnp.exp2(log_parts - jnp.max(log_parts, axis=0)[None])
        factor = factor * (1.0 / jnp.sum(factor, axis=0))[None]
        data = part_in[:, r].astype(F32)
        att.append([jnp.sum(data[:, 8 * u : 8 * u + 8] * factor, axis=0) for u in range(2)])
    pieces = []
    for c in range(4):
        lo, hi = att[0][c // 2], att[1][c // 2]
        if c % 2 == 0:
            pieces.append(jnp.where(sub < 4, lo, pltpu.roll(hi, 4, 0)))
        else:
            pieces.append(jnp.where(sub < 4, pltpu.roll(lo, 4, 0), hi))
    attended = jnp.concatenate(pieces, axis=1).astype(BF16)
    values = []
    for h in range(4):
        got = dot(attended, uv[h])
        values.append(jnp.where(sub % 2 == 0, got[h : h + 1], got[4 + h : 5 + h]))
    head_values = jnp.concatenate(values, axis=1).astype(BF16)
    weights[1].wait()
    partial = dot(head_values, wo[...])
    for j in range(REDUCERS):
        attn_out[j] = packed(partial, j)

    for chip in chips:

        @pl.when(jnp.logical_and(chip < REDUCERS, k != 2 * chip))
        def _(chip=chip):
            send(attn_out.at[chip], attn_in.at[k], 2, plane + 2 * chip)

    reducer = jnp.logical_and(k % 2 == 0, k < 2 * REDUCERS)

    @pl.when(reducer)
    def _():
        j = own_chip
        attn_in[k] = attn_out[j]
        own_hid = hid_tiles[j]
        wait_for(recv_sem.at[2], attn_in, KV - 1)
        mine = (jnp.sum(attn_in[...], axis=0) + own_hid).astype(BF16).astype(F32)
        row_tiles[z] = mine
        stream_own[...] = mine
        send_row(stream_own, row_tiles.at[z], 3)
        wait_for(recv_sem.at[3], row_tiles, ROWS - 1)
        tiles = []
        for c in range(4):
            tile = None
            for zz in range(ROWS):
                shift = (2 * zz - 2 * c) % 8
                piece = row_tiles[zz]
                if shift:
                    piece = pltpu.roll(piece, shift, 0)
                tile = piece if tile is None else jnp.where(sub // 2 == zz, piece, tile)
            tiles.append(tile)
        for u in range(2):
            both = jnp.concatenate(tiles[2 * u : 2 * u + 2], axis=0).astype(BF16)
            wide[u] = both
            stream_all[j, u] = both
        send_kv(lambda peer: wide, stream_all.at[j], 4)
        wait_for(recv_sem.at[4], stream_all, REDUCERS - 1)

    @pl.when(jnp.logical_not(reducer))
    def _():
        wait_for(recv_sem.at[4], stream_all, REDUCERS)

    parts = stream_all[...].astype(F32)
    stream = jnp.concatenate(
        [parts[t // 4, (t // 2) % 2, 8 * (t % 2) : 8 * (t % 2) + 8] for t in range(D // 128)], axis=1
    )
    mean_sq = jnp.sum(stream * stream, axis=1, keepdims=True) * (1.0 / D)
    normed = (stream * lax.rsqrt(mean_sq + 1e-06) * gain[...].astype(F32).reshape(1, D)).astype(BF16)
    for copy in weights[2:4]:
        copy.wait()
    gate_proj = dot(normed, wg[...], ((1,), (1,)))
    up_proj = dot(normed, wu[...], ((1,), (1,)))
    hidden = (gate_proj / (1.0 + jnp.exp(-gate_proj)) * up_proj).astype(BF16)
    weights[4].wait()
    down = dot(hidden, wd[...])
    down = jnp.concatenate([down, jnp.zeros((8, 128), F32)], axis=1)
    for p in range(KV):
        tile, shift = divmod(OUT_COLS * p, 128)
        three = [down[:, 128 * (tile + i) : 128 * (tile + i + 1)] for i in range(3)]
        if shift:
            turned = [pltpu.roll(t, 128 - shift, 1) for t in three]
            two = [jnp.where(lane < 128 - shift, turned[i], turned[i + 1]) for i in range(2)]
        else:
            two = three[:2]
        down_out[p] = jnp.concatenate(two, axis=0).astype(BF16)
    down_in[k] = down_out[k]
    send_kv(lambda peer: down_out.at[peer], down_in.at[k], 5)

    own_tile = lax.div(7 * k, 4)
    wide_stream[:, pl.ds(0, D)] = stream
    wide_stream[:, pl.ds(D, 512)] = jnp.zeros((8, 512), F32)
    own_stream = wide_stream[:, pl.ds(pl.multiple_of(own_tile * 128, 128), 512)]
    own_stream = pltpu.roll(own_stream, lax.rem(512 - (OUT_COLS * k - 128 * own_tile), 512), 1)[:, :256]

    wait_for(recv_sem.at[5], down_in, KV - 1)
    mine = jnp.sum(down_in[...].astype(F32), axis=0)
    last_own[...] = mine
    last_in[z] = mine
    send_row(last_own, last_in.at[z], 6)
    wait_for(recv_sem.at[6], last_in, ROWS - 1)
    final = jnp.sum(last_in[...], axis=0)
    result = jnp.concatenate([final[0:8], final[8:16]], axis=1) + own_stream
    own = result[0:2]
    for zz in range(1, ROWS):
        own = jnp.where(z == zz, result[2 * zz : 2 * zz + 2], own)
    out_ref[...] = own[:, :OUT_COLS]

    for i, buffer in ((1, part_in), (5, down_in)):
        wait_for(send_sem.at[i], buffer, KV - 1)
    wait_for(send_sem.at[6], last_in, ROWS - 1)

    @pl.when(reducer)
    def _():
        wait_for(send_sem.at[2], attn_out, REDUCERS - 1)
        wait_for(send_sem.at[3], row_tiles, ROWS - 1)
        sent = s.at[0, pl.ds(0, 16), pl.ds(0, 128 * (KV - 1))]
        pltpu.make_async_copy(sent, sent, send_sem.at[4]).wait()

    @pl.when(jnp.logical_not(reducer))
    def _():
        wait_for(send_sem.at[2], attn_out, REDUCERS)


def body(query, latent_cache, new_latent, lengths, w_uv, w_o, hidden_in, norm_gain, w_gate, w_up, w_down):
    anywhere = pl.BlockSpec(memory_space=pl.ANY)
    vmem = pltpu.VMEM
    return pl.pallas_call(
        kernel,
        out_shape=jax.ShapeDtypeStruct((HERE, OUT_COLS), F32),
        in_specs=[anywhere] * 3 + [pl.BlockSpec(memory_space=pltpu.SMEM)] + [anywhere] * 7,
        out_specs=pl.BlockSpec(memory_space=vmem),
        scratch_shapes=[
            vmem((HERE, QK, HEADS), BF16),
            vmem((HERE, QK, SPAN), BF16),
            vmem((HERE, QK), BF16),
            vmem((4, LATENT, HEAD_DIM), BF16),
            vmem((4 * HEAD_DIM, D), BF16),
            vmem((HERE, D), BF16),
            vmem((D,), BF16),
            vmem((LOCAL_FF, D), BF16),
            vmem((LOCAL_FF, D), BF16),
            vmem((LOCAL_FF, D), BF16),
            vmem((HERE, HEADS, QK), BF16),
            vmem((HERE, HEADS, SPAN), F32),
            vmem((HERE, HEADS, SPAN), BF16),
            vmem((HERE, LATENT, HEADS), F32),
            vmem((REDUCERS, 8, 128), F32),
            vmem((KV // 2, 2, HERE + 1, 16, 128), BF16),
            vmem((KV, HERE + 1, 16, 128), BF16),
            vmem((REDUCERS, 8, 128), F32),
            vmem((KV, 8, 128), F32),
            vmem((ROWS, 8, 128), F32),
            vmem((8, 128), F32),
            vmem((REDUCERS, 2, 16, 128), BF16),
            vmem((2, 16, 128), BF16),
            vmem((KV, 16, 128), BF16),
            vmem((KV, 16, 128), BF16),
            vmem((16, 128), F32),
            vmem((ROWS, 16, 128), F32),
            vmem((8, D + 512), F32),
            pltpu.SemaphoreType.DMA((9,)),
            pltpu.SemaphoreType.DMA((HERE, 3)),
            pltpu.SemaphoreType.DMA((7,)),
            pltpu.SemaphoreType.DMA((7,)),
        ],
        compiler_params=pltpu.CompilerParams(
            collective_id=0, has_side_effects=True, vmem_limit_bytes=60 * 1024 * 1024
        ),
    )(
        jnp.swapaxes(query, 1, 2),
        jnp.swapaxes(latent_cache, 1, 2),
        new_latent,
        lengths,
        w_uv,
        w_o,
        hidden_in,
        norm_gain,
        w_gate.T,
        w_up.T,
        w_down,
    )


def solution(mesh):
    placed = (
        P("row", None, None),
        P("row", "kv", None),
        P("row", None),
        P("row"),
        P("kv", None, None),
        P("kv", None),
        P("row", None),
        P(),
        P(None, ("row", "kv")),
        P(None, ("row", "kv")),
        P(("row", "kv"), None),
    )
    return jax.shard_map(body, mesh=mesh, in_specs=placed, out_specs=P("row", "kv"), check_vma=False)
```

```python
import jax
import jax.numpy as jnp
from jax import lax
from jax.experimental import pallas as pl
from jax.experimental.pallas import tpu as pltpu
from jax.sharding import PartitionSpec as P

LOGICAL = pl.DeviceIdType.LOGICAL
F32, BF16 = jnp.float32, jnp.bfloat16

HEADS, LATENT, ROPE, HEAD_DIM, QK = 128, 512, 64, 128, 576
D, LOCAL_FF, SPAN = 7168, 144, 5120
KV, ROWS, HERE = 32, 4, 2
OUT_COLS = D // KV
CHUNK = 1024
BLOCK = 256
CHUNKS = SPAN // CHUNK
REDUCERS = 14
LOG2E = 1.4426950408889634
SCALE2 = LOG2E * (HEAD_DIM + ROPE) ** -0.5
NEG_FILL = -1e30


def dot(a, b, dims=((1,), (0,))):
    return lax.dot_general(a, b, (dims, ((), ())), preferred_element_type=F32)


def kernel(
    q_hbm, cache_hbm, new_hbm, lengths_ref, uv_hbm, wo_hbm, hid_hbm, gain_hbm, gate_hbm, up_hbm, down_hbm,
    out_ref,
    qt, kt, new, uv, wo, hid_in, gain, wg, wu, wd,
    q, s, w, hid_tiles,
    log_out, log_in, part_out, part_in, attn_out, attn_in, row_tiles, stream_own, stream_all, wide,
    down_out, down_in, last_own, last_in, wide_stream,
    in_sem, cache_sem, send_sem, recv_sem,
):
    k = lax.axis_index("kv")
    z = lax.axis_index("row")

    small = [
        pltpu.make_async_copy(src, dst, in_sem.at[i])
        for i, (src, dst) in enumerate(((q_hbm, qt), (new_hbm, new), (hid_hbm, hid_in), (gain_hbm, gain)))
    ]
    for copy in small:
        copy.start()
    cache = [
        [
            pltpu.make_async_copy(
                cache_hbm.at[r, :, pl.ds(c * CHUNK, CHUNK)], kt.at[r, :, pl.ds(c * CHUNK, CHUNK)], cache_sem.at[r, c]
            )
            for c in range(CHUNKS)
        ]
        for r in range(HERE)
    ]
    for r in range(HERE):
        for c in range(CHUNKS):
            cache[r][c].start()
    weights = [
        pltpu.make_async_copy(src, dst, in_sem.at[4 + i])
        for i, (src, dst) in enumerate(((uv_hbm, uv), (wo_hbm, wo), (gate_hbm, wg), (up_hbm, wu), (down_hbm, wd)))
    ]

    barrier = pltpu.get_barrier_semaphore()

    plane = z * KV
    own_chip, own_core = lax.div(k, 2), lax.rem(k, 2)
    xs = [4 * lax.rem(lax.div(own_chip, 4) + d, 4) for d in range(4)]
    ys = [lax.rem(lax.rem(own_chip, 4) + d, 4) for d in range(4)]
    cores = [own_core, 1 - own_core]
    offsets = sorted(((dx, dy) for dx in range(4) for dy in range(4)), key=lambda o: -min(o[0], 4 - o[0]) - min(o[1], 4 - o[1]))
    chips = [xs[dx] + ys[dy] for dx, dy in offsets]
    peers = [2 * chip + core for chip in chips for core in cores]
    del peers[-2]
    row_peers = [lax.rem(z + d, ROWS) * KV + k for d in (2, 1, 3)]
    for peer in [plane + p for p in peers] + row_peers:
        pl.semaphore_signal(barrier, inc=1, device_id=peer, device_id_type=LOGICAL)

    def send(src, dst, lane, device):
        pltpu.make_async_remote_copy(
            src_ref=src, dst_ref=dst, send_sem=send_sem.at[lane], recv_sem=recv_sem.at[lane],
            device_id=device, device_id_type=LOGICAL,
        ).start()

    def send_kv(src, dst, lane):
        for peer in peers:
            send(src(peer), dst, lane, plane + peer)

    def send_row(src, dst, lane):
        for peer in row_peers:
            send(src, dst, lane, peer)

    def wait_for(sem, buffer, count):
        span = buffer.at[pl.ds(0, count)]
        pltpu.make_async_copy(span, span, sem).wait()

    sub = lax.broadcasted_iota(jnp.int32, (8, 128), 0)
    lane = lax.broadcasted_iota(jnp.int32, (8, 128), 1)

    small[0].wait()
    for r in range(HERE):
        q[r] = qt[r].astype(F32).T.astype(BF16)

    def packed(rows, j):
        base = 512 * j
        tile = rows[:, base : base + 128]
        for c in range(1, 4):
            tile = jnp.where(sub // 2 == c, rows[:, base + 128 * c : base + 128 * (c + 1)], tile)
        return tile

    position = lax.broadcasted_iota(jnp.int32, (1, BLOCK), 1) + k * SPAN

    def scores(r, c):
        cache[r][c].wait()
        most = None
        for first in range(c * CHUNK, (c + 1) * CHUNK, BLOCK):
            cols = pl.ds(first, BLOCK)
            raw = dot(q[r], kt[r, :, cols]) * SCALE2
            raw = jnp.where(position + first < lengths_ref[r], raw, NEG_FILL)
            s[r, :, cols] = raw
            for part in range(0, BLOCK, 128):
                piece = raw[:, part : part + 128]
                most = piece if most is None else jnp.maximum(most, piece)
        return most

    def weigh(r, c, top):
        cols = pl.ds(c * CHUNK, CHUNK)
        value = jnp.exp2(s[r, :, cols] - top)
        w[r, :, cols] = value.astype(BF16)
        added = value[:, :128]
        for part in range(128, CHUNK, 128):
            added = added + value[:, part : part + 128]
        return added

    def highest(r, parts):
        most = parts[0]
        for part in parts[1:]:
            most = jnp.maximum(most, part)
        new_score = jnp.sum(q[r].astype(F32) * new[r : r + 1, :].astype(F32), axis=1, keepdims=True) * SCALE2
        return new_score, jnp.maximum(jnp.max(most, axis=1, keepdims=True), new_score)

    def summed(parts):
        added = parts[0]
        for part in parts[1:]:
            added = added + part
        return jnp.sum(added, axis=1, keepdims=True)

    parts = [scores(0, c) for c in range(CHUNKS)]
    small[1].wait()
    new0, top0 = highest(0, parts)
    weights[0].start()
    weights[1].start()
    parts, sums = [], []
    for c in range(CHUNKS):
        parts.append(scores(1, c))
        sums.append(weigh(0, c, top0))
    for copy in weights[2:]:
        copy.start()
    new1, top1 = highest(1, parts)
    new_score, top = [new0, new1], [top0, top1]
    total = [summed(sums), summed([weigh(1, c, top1) for c in range(CHUNKS)])]
    half = lax.broadcasted_iota(jnp.int32, (16, 8, 128), 1) < 4
    left = lax.broadcasted_iota(jnp.int32, (HEADS, 128), 1) < 64
    wide_zero = jnp.zeros((HEADS, 128), F32)

    def share(first, second):
        t0, t1 = first.reshape(16, 8, 128), second.reshape(16, 8, 128)
        return jnp.where(half, t0, pltpu.roll(t1, 4, 1)), jnp.where(half, pltpu.roll(t0, 4, 1), t1)

    def rounded(value):
        return value.astype(BF16).astype(F32)

    logs, norms, own_news = [], [], []
    for r in range(HERE):
        own_new = jnp.where(k == 0, jnp.exp2(new_score[r] - top[r]), 0.0)
        norm = jnp.maximum(total[r] + own_new, 1e-30)
        log_total = top[r] + jnp.log(norm) * LOG2E
        high = rounded(log_total)
        middle = rounded(log_total - high)
        low = log_total - high - middle
        logs.append(share(jnp.where(left, high, middle), jnp.where(left, low, wide_zero)))
        norms.append(norm)
        own_news.append(own_new)
    for core in range(2):
        log_out[:, core] = jnp.concatenate([logs[0][core], logs[1][core]], axis=1).astype(BF16)
    pl.semaphore_wait(barrier, KV - 1 + ROWS - 1)
    send_kv(lambda peer: log_out.at[lax.div(peer, 2), lax.rem(peer, 2)], log_in.at[k], 0)
    log_in[k] = log_out[own_chip, own_core]

    for r in range(HERE):
        value = dot(kt[r, :LATENT, :], w[r], ((1,), (1,))).T
        mine = (value + own_news[r] * new[r : r + 1, :LATENT].astype(F32)) * (1.0 / norms[r])
        quarters = [mine[:, 128 * c : 128 * c + 128] for c in range(4)]
        both = [share(quarters[2 * u], quarters[2 * u + 1]) for u in range(2)]
        for core in range(2):
            part_out[r, :, core] = jnp.concatenate([both[0][core], both[1][core]], axis=1).astype(BF16)
        send_kv(lambda peer: part_out.at[r, lax.div(peer, 2), lax.rem(peer, 2)], part_in.at[r, k], 1 + 6 * r)
        part_in[r, k] = part_out[r, own_chip, own_core]

    for copy in small[2:]:
        copy.wait()
    hid_f = hid_in[...].astype(F32)
    hid_rows = jnp.where(lax.broadcasted_iota(jnp.int32, (8, D), 0) % 2 == 0, hid_f[0:1], hid_f[1:2])

    for j in range(REDUCERS):
        hid_tiles[j] = packed(hid_rows, j)

    weights[0].wait()
    wait_for(recv_sem.at[0], log_in, KV - 1)
    att = []
    for r in range(HERE):
        log_parts = log_in[:, 8 * r : 8 * r + 8].astype(F32)
        log_parts = log_parts + pltpu.roll(log_parts, 64, 2)
        log_parts = log_parts + pltpu.roll(log_parts, 4, 1)
        factor = jnp.exp2(log_parts - jnp.max(log_parts, axis=0)[None])
        factor = factor * (1.0 / jnp.sum(factor, axis=0))[None]
        wait_for(recv_sem.at[1 + 6 * r], part_in.at[r], KV - 1)
        data = part_in[r].astype(F32)
        att.append([jnp.sum(data[:, 8 * u : 8 * u + 8] * factor, axis=0) for u in range(2)])
    pieces = []
    for c in range(4):
        lo, hi = att[0][c // 2], att[1][c // 2]
        if c % 2 == 0:
            pieces.append(jnp.where(sub < 4, lo, pltpu.roll(hi, 4, 0)))
        else:
            pieces.append(jnp.where(sub < 4, pltpu.roll(lo, 4, 0), hi))
    attended = jnp.concatenate(pieces, axis=1).astype(BF16)
    values = []
    for h in range(4):
        got = dot(attended, uv[h])
        values.append(jnp.where(sub % 2 == 0, got[h : h + 1], got[4 + h : 5 + h]))
    head_values = jnp.concatenate(values, axis=1).astype(BF16)
    weights[1].wait()
    partial = dot(head_values, wo[...])
    for j in range(REDUCERS):
        attn_out[j] = packed(partial, j)

    for chip in chips:

        @pl.when(jnp.logical_and(chip < REDUCERS, k != 2 * chip))
        def _(chip=chip):
            send(attn_out.at[chip], attn_in.at[k], 2, plane + 2 * chip)

    reducer = jnp.logical_and(k % 2 == 0, k < 2 * REDUCERS)

    @pl.when(reducer)
    def _():
        j = own_chip
        attn_in[k] = attn_out[j]
        own_hid = hid_tiles[j]
        wait_for(recv_sem.at[2], attn_in, KV - 1)
        mine = (jnp.sum(attn_in[...], axis=0) + own_hid).astype(BF16).astype(F32)
        row_tiles[z] = mine
        stream_own[...] = mine
        send_row(stream_own, row_tiles.at[z], 3)
        wait_for(recv_sem.at[3], row_tiles, ROWS - 1)
        tiles = []
        for c in range(4):
            tile = None
            for zz in range(ROWS):
                shift = (2 * zz - 2 * c) % 8
                piece = row_tiles[zz]
                if shift:
                    piece = pltpu.roll(piece, shift, 0)
                tile = piece if tile is None else jnp.where(sub // 2 == zz, piece, tile)
            tiles.append(tile)
        for u in range(2):
            both = jnp.concatenate(tiles[2 * u : 2 * u + 2], axis=0).astype(BF16)
            wide[u] = both
            stream_all[j, u] = both
        send_kv(lambda peer: wide, stream_all.at[j], 4)
        wait_for(recv_sem.at[4], stream_all, REDUCERS - 1)

    @pl.when(jnp.logical_not(reducer))
    def _():
        wait_for(recv_sem.at[4], stream_all, REDUCERS)

    parts = stream_all[...].astype(F32)
    stream = jnp.concatenate(
        [parts[t // 4, (t // 2) % 2, 8 * (t % 2) : 8 * (t % 2) + 8] for t in range(D // 128)], axis=1
    )
    mean_sq = jnp.sum(stream * stream, axis=1, keepdims=True) * (1.0 / D)
    normed = (stream * lax.rsqrt(mean_sq + 1e-06) * gain[...].astype(F32).reshape(1, D)).astype(BF16)
    for copy in weights[2:4]:
        copy.wait()
    gate_proj = dot(normed, wg[...], ((1,), (1,)))
    up_proj = dot(normed, wu[...], ((1,), (1,)))
    hidden = (gate_proj / (1.0 + jnp.exp(-gate_proj)) * up_proj).astype(BF16)
    weights[4].wait()
    down = dot(hidden, wd[...])
    down = jnp.concatenate([down, jnp.zeros((8, 128), F32)], axis=1)
    for p in range(KV):
        tile, shift = divmod(OUT_COLS * p, 128)
        three = [down[:, 128 * (tile + i) : 128 * (tile + i + 1)] for i in range(3)]
        if shift:
            turned = [pltpu.roll(t, 128 - shift, 1) for t in three]
            two = [jnp.where(lane < 128 - shift, turned[i], turned[i + 1]) for i in range(2)]
        else:
            two = three[:2]
        down_out[p] = jnp.concatenate(two, axis=0).astype(BF16)
    down_in[k] = down_out[k]
    send_kv(lambda peer: down_out.at[peer], down_in.at[k], 5)

    own_tile = lax.div(7 * k, 4)
    wide_stream[:, pl.ds(0, D)] = stream
    wide_stream[:, pl.ds(D, 512)] = jnp.zeros((8, 512), F32)
    own_stream = wide_stream[:, pl.ds(pl.multiple_of(own_tile * 128, 128), 512)]
    own_stream = pltpu.roll(own_stream, lax.rem(512 - (OUT_COLS * k - 128 * own_tile), 512), 1)[:, :256]

    wait_for(recv_sem.at[5], down_in, KV - 1)
    mine = jnp.sum(down_in[...].astype(F32), axis=0)
    last_own[...] = mine
    last_in[z] = mine
    send_row(last_own, last_in.at[z], 6)
    wait_for(recv_sem.at[6], last_in, ROWS - 1)
    final = jnp.sum(last_in[...], axis=0)
    result = jnp.concatenate([final[0:8], final[8:16]], axis=1) + own_stream
    own = result[0:2]
    for zz in range(1, ROWS):
        own = jnp.where(z == zz, result[2 * zz : 2 * zz + 2], own)
    out_ref[...] = own[:, :OUT_COLS]

    for i, buffer in ((0, log_in), (1, part_in.at[0]), (7, part_in.at[1]), (5, down_in)):
        wait_for(send_sem.at[i], buffer, KV - 1)
    wait_for(send_sem.at[6], last_in, ROWS - 1)

    @pl.when(reducer)
    def _():
        wait_for(send_sem.at[2], attn_out, REDUCERS - 1)
        wait_for(send_sem.at[3], row_tiles, ROWS - 1)
        sent = s.at[0, pl.ds(0, 16), pl.ds(0, 128 * (KV - 1))]
        pltpu.make_async_copy(sent, sent, send_sem.at[4]).wait()

    @pl.when(jnp.logical_not(reducer))
    def _():
        wait_for(send_sem.at[2], attn_out, REDUCERS)


def body(query, latent_cache, new_latent, lengths, w_uv, w_o, hidden_in, norm_gain, w_gate, w_up, w_down):
    anywhere = pl.BlockSpec(memory_space=pl.ANY)
    vmem = pltpu.VMEM
    return pl.pallas_call(
        kernel,
        out_shape=jax.ShapeDtypeStruct((HERE, OUT_COLS), F32),
        in_specs=[anywhere] * 3 + [pl.BlockSpec(memory_space=pltpu.SMEM)] + [anywhere] * 7,
        out_specs=pl.BlockSpec(memory_space=vmem),
        scratch_shapes=[
            vmem((HERE, QK, HEADS), BF16),
            vmem((HERE, QK, SPAN), BF16),
            vmem((HERE, QK), BF16),
            vmem((4, LATENT, HEAD_DIM), BF16),
            vmem((4 * HEAD_DIM, D), BF16),
            vmem((HERE, D), BF16),
            vmem((D,), BF16),
            vmem((LOCAL_FF, D), BF16),
            vmem((LOCAL_FF, D), BF16),
            vmem((LOCAL_FF, D), BF16),
            vmem((HERE, HEADS, QK), BF16),
            vmem((HERE, HEADS, SPAN), F32),
            vmem((HERE, HEADS, SPAN), BF16),
            vmem((REDUCERS, 8, 128), F32),
            vmem((KV // 2, 2, 16, 128), BF16),
            vmem((KV, 16, 128), BF16),
            vmem((HERE, KV // 2, 2, 16, 128), BF16),
            vmem((HERE, KV, 16, 128), BF16),
            vmem((REDUCERS, 8, 128), F32),
            vmem((KV, 8, 128), F32),
            vmem((ROWS, 8, 128), F32),
            vmem((8, 128), F32),
            vmem((REDUCERS, 2, 16, 128), BF16),
            vmem((2, 16, 128), BF16),
            vmem((KV, 16, 128), BF16),
            vmem((KV, 16, 128), BF16),
            vmem((16, 128), F32),
            vmem((ROWS, 16, 128), F32),
            vmem((8, D + 512), F32),
            pltpu.SemaphoreType.DMA((9,)),
            pltpu.SemaphoreType.DMA((HERE, CHUNKS)),
            pltpu.SemaphoreType.DMA((8,)),
            pltpu.SemaphoreType.DMA((8,)),
        ],
        compiler_params=pltpu.CompilerParams(
            collective_id=0, has_side_effects=True, vmem_limit_bytes=60 * 1024 * 1024
        ),
    )(
        jnp.swapaxes(query, 1, 2),
        jnp.swapaxes(latent_cache, 1, 2),
        new_latent,
        lengths,
        w_uv,
        w_o,
        hidden_in,
        norm_gain,
        w_gate.T,
        w_up.T,
        w_down,
    )


def solution(mesh):
    placed = (
        P("row", None, None),
        P("row", "kv", None),
        P("row", None),
        P("row"),
        P("kv", None, None),
        P("kv", None),
        P("row", None),
        P(),
        P(None, ("row", "kv")),
        P(None, ("row", "kv")),
        P(("row", "kv"), None),
    )
    return jax.shard_map(body, mesh=mesh, in_specs=placed, out_specs=P("row", "kv"), check_vma=False)
```

```python
import jax
import jax.numpy as jnp
from jax import lax
from jax.experimental import pallas as pl
from jax.experimental.pallas import tpu as pltpu
from jax.sharding import PartitionSpec as P

LOGICAL = pl.DeviceIdType.LOGICAL
F32, BF16 = jnp.float32, jnp.bfloat16

HEADS, LATENT, ROPE, HEAD_DIM, QK = 128, 512, 64, 128, 576
D, LOCAL_FF, SPAN = 7168, 144, 5120
KV, ROWS, HERE = 32, 4, 2
OUT_COLS = D // KV
CHUNK = 1024
BLOCK = 256
CHUNKS = SPAN // CHUNK
REDUCERS = 14
LOG2E = 1.4426950408889634
SCALE2 = LOG2E * (HEAD_DIM + ROPE) ** -0.5
NEG_FILL = -1e30


def dot(a, b, dims=((1,), (0,))):
    return lax.dot_general(a, b, (dims, ((), ())), preferred_element_type=F32)


def kernel(
    q_hbm, cache_hbm, new_hbm, lengths_ref, uv_hbm, wo_hbm, hid_hbm, gain_hbm, gate_hbm, up_hbm, down_hbm,
    out_ref,
    qt, kt, new, uv, wo, hid_in, gain, wg, wu, wd,
    q, s, w, acc, hid_tiles,
    part_out, part_in, attn_out, attn_in, row_tiles, stream_own, stream_all, wide,
    down_out, down_in, last_own, last_in, wide_stream,
    in_sem, cache_sem, send_sem, recv_sem, stream_sem,
):
    k = lax.axis_index("kv")
    z = lax.axis_index("row")

    small = [
        pltpu.make_async_copy(src, dst, in_sem.at[i])
        for i, (src, dst) in enumerate(((q_hbm, qt), (new_hbm, new), (hid_hbm, hid_in), (gain_hbm, gain)))
    ]
    for copy in small:
        copy.start()
    cache = [
        [
            pltpu.make_async_copy(
                cache_hbm.at[r, :, pl.ds(c * CHUNK, CHUNK)], kt.at[r, :, pl.ds(c * CHUNK, CHUNK)], cache_sem.at[r, c]
            )
            for c in range(CHUNKS)
        ]
        for r in range(HERE)
    ]
    for r in range(HERE):
        for c in range(CHUNKS):
            cache[r][c].start()
    weights = [
        pltpu.make_async_copy(src, dst, in_sem.at[4 + i])
        for i, (src, dst) in enumerate(((uv_hbm, uv), (wo_hbm, wo), (gate_hbm, wg), (up_hbm, wu), (down_hbm, wd)))
    ]

    barrier = pltpu.get_barrier_semaphore()

    plane = z * KV
    own_chip, own_core = lax.div(k, 2), lax.rem(k, 2)
    xs = [4 * lax.rem(lax.div(own_chip, 4) + d, 4) for d in range(4)]
    ys = [lax.rem(lax.rem(own_chip, 4) + d, 4) for d in range(4)]
    cores = [own_core, 1 - own_core]
    offsets = sorted(((dx, dy) for dx in range(4) for dy in range(4)), key=lambda o: -min(o[0], 4 - o[0]) - min(o[1], 4 - o[1]))
    chips = [xs[dx] + ys[dy] for dx, dy in offsets]
    peers = [2 * chip + core for chip in chips for core in cores]
    del peers[-2]
    row_peers = [lax.rem(z + d, ROWS) * KV + k for d in (2, 1, 3)]
    for peer in [plane + p for p in peers] + row_peers:
        pl.semaphore_signal(barrier, inc=1, device_id=peer, device_id_type=LOGICAL)

    def send(src, dst, lane, device):
        pltpu.make_async_remote_copy(
            src_ref=src, dst_ref=dst, send_sem=send_sem.at[lane], recv_sem=recv_sem.at[lane],
            device_id=device, device_id_type=LOGICAL,
        ).start()

    def send_kv(src, dst, lane):
        for peer in peers:
            send(src(peer), dst, lane, plane + peer)

    def send_row(src, dst, lane):
        for peer in row_peers:
            send(src, dst, lane, peer)

    def wait_for(sem, buffer, count):
        span = buffer.at[pl.ds(0, count)]
        pltpu.make_async_copy(span, span, sem).wait()

    sub = lax.broadcasted_iota(jnp.int32, (8, 128), 0)
    lane = lax.broadcasted_iota(jnp.int32, (8, 128), 1)

    small[0].wait()
    for r in range(HERE):
        q[r] = qt[r].astype(F32).T.astype(BF16)

    def packed(rows, j):
        base = 512 * j
        tile = rows[:, base : base + 128]
        for c in range(1, 4):
            tile = jnp.where(sub // 2 == c, rows[:, base + 128 * c : base + 128 * (c + 1)], tile)
        return tile

    position = lax.broadcasted_iota(jnp.int32, (1, BLOCK), 1) + k * SPAN

    def scores(r, c):
        cache[r][c].wait()
        most = None
        for first in range(c * CHUNK, (c + 1) * CHUNK, BLOCK):
            cols = pl.ds(first, BLOCK)
            raw = dot(q[r], kt[r, :, cols]) * SCALE2
            raw = jnp.where(position + first < lengths_ref[r], raw, NEG_FILL)
            s[r, :, cols] = raw
            for part in range(0, BLOCK, 128):
                piece = raw[:, part : part + 128]
                most = piece if most is None else jnp.maximum(most, piece)
        return most

    def weigh(r, c, top):
        cols = pl.ds(c * CHUNK, CHUNK)
        value = jnp.exp2(s[r, :, cols] - top)
        w[r, :, cols] = value.astype(BF16)
        added = value[:, :128]
        for part in range(128, CHUNK, 128):
            added = added + value[:, part : part + 128]
        return added

    def highest(r, parts):
        most = parts[0]
        for part in parts[1:]:
            most = jnp.maximum(most, part)
        new_score = jnp.sum(q[r].astype(F32) * new[r : r + 1, :].astype(F32), axis=1, keepdims=True) * SCALE2
        return new_score, jnp.maximum(jnp.max(most, axis=1, keepdims=True), new_score)

    def summed(parts):
        added = parts[0]
        for part in parts[1:]:
            added = added + part
        return jnp.sum(added, axis=1, keepdims=True)

    parts = [scores(0, c) for c in range(CHUNKS)]
    small[1].wait()
    new0, top0 = highest(0, parts)
    weights[0].start()
    weights[1].start()
    parts, sums = [], []
    for c in range(CHUNKS):
        parts.append(scores(1, c))
        sums.append(weigh(0, c, top0))
    for copy in weights[2:]:
        copy.start()
    new1, top1 = highest(1, parts)
    new_score, top = [new0, new1], [top0, top1]
    total = [summed(sums), summed([weigh(1, c, top1) for c in range(CHUNKS)])]
    for r in range(HERE):
        acc[r] = dot(kt[r, :LATENT, :], w[r], ((1,), (1,)))

    half = lax.broadcasted_iota(jnp.int32, (16, 8, 128), 1) < 4
    left = lax.broadcasted_iota(jnp.int32, (HEADS, 128), 1) < 64
    wide_zero = jnp.zeros((HEADS, 128), F32)

    def share(first, second):
        t0, t1 = first.reshape(16, 8, 128), second.reshape(16, 8, 128)
        return jnp.where(half, t0, pltpu.roll(t1, 4, 1)), jnp.where(half, pltpu.roll(t0, 4, 1), t1)

    def rounded(value):
        return value.astype(BF16).astype(F32)

    logs = []
    for r in range(HERE):
        own_new = jnp.where(k == 0, jnp.exp2(new_score[r] - top[r]), 0.0)
        norm = jnp.maximum(total[r] + own_new, 1e-30)
        log_total = top[r] + jnp.log(norm) * LOG2E
        high = rounded(log_total)
        middle = rounded(log_total - high)
        low = log_total - high - middle
        logs.append(share(jnp.where(left, high, middle), jnp.where(left, low, wide_zero)))
        mine = (acc[r].T + own_new * new[r : r + 1, :LATENT].astype(F32)) * (1.0 / norm)
        quarters = [mine[:, 128 * c : 128 * c + 128] for c in range(4)]
        both = [share(quarters[2 * u], quarters[2 * u + 1]) for u in range(2)]
        for core in range(2):
            part_out[:, core, r] = jnp.concatenate([both[0][core], both[1][core]], axis=1).astype(BF16)
    for core in range(2):
        part_out[:, core, HERE] = jnp.concatenate([logs[0][core], logs[1][core]], axis=1).astype(BF16)
    pl.semaphore_wait(barrier, KV - 1 + ROWS - 1)
    send_kv(lambda peer: part_out.at[lax.div(peer, 2), lax.rem(peer, 2)], part_in.at[k], 1)
    part_in[k] = part_out[own_chip, own_core]

    for copy in small[2:]:
        copy.wait()
    hid_f = hid_in[...].astype(F32)
    hid_rows = jnp.where(lax.broadcasted_iota(jnp.int32, (8, D), 0) % 2 == 0, hid_f[0:1], hid_f[1:2])

    for j in range(REDUCERS):
        hid_tiles[j] = packed(hid_rows, j)

    wait_for(recv_sem.at[1], part_in, KV - 1)
    weights[0].wait()
    att = []
    for r in range(HERE):
        log_parts = part_in[:, HERE, 8 * r : 8 * r + 8].astype(F32)
        log_parts = log_parts + pltpu.roll(log_parts, 64, 2)
        log_parts = log_parts + pltpu.roll(log_parts, 4, 1)
        factor = jnp.exp2(log_parts - jnp.max(log_parts, axis=0)[None])
        factor = factor * (1.0 / jnp.sum(factor, axis=0))[None]
        data = part_in[:, r].astype(F32)
        att.append([jnp.sum(data[:, 8 * u : 8 * u + 8] * factor, axis=0) for u in range(2)])
    pieces = []
    for c in range(4):
        lo, hi = att[0][c // 2], att[1][c // 2]
        if c % 2 == 0:
            pieces.append(jnp.where(sub < 4, lo, pltpu.roll(hi, 4, 0)))
        else:
            pieces.append(jnp.where(sub < 4, pltpu.roll(lo, 4, 0), hi))
    attended = jnp.concatenate(pieces, axis=1).astype(BF16)
    values = []
    for h in range(4):
        got = dot(attended, uv[h])
        values.append(jnp.where(sub % 2 == 0, got[h : h + 1], got[4 + h : 5 + h]))
    head_values = jnp.concatenate(values, axis=1).astype(BF16)
    weights[1].wait()
    for low in (0, 7):
        partial = dot(head_values, wo[:, 512 * low : 512 * (low + 7)])
        for j in range(7):
            attn_out[low + j] = packed(partial, j)
        for chip in chips:

            @pl.when(jnp.logical_and(jnp.logical_and(chip >= low, chip < low + 7), k != 2 * chip))
            def _(chip=chip):
                send(attn_out.at[chip], attn_in.at[k], 2, plane + 2 * chip)

    reducer = jnp.logical_and(k % 2 == 0, k < 2 * REDUCERS)

    @pl.when(reducer)
    def _():
        j = own_chip
        attn_in[k] = attn_out[j]
        own_hid = hid_tiles[j]
        wait_for(recv_sem.at[2], attn_in, KV - 1)
        mine = (jnp.sum(attn_in[...], axis=0) + own_hid).astype(BF16).astype(F32)
        row_tiles[z] = mine
        stream_own[...] = mine
        send_row(stream_own, row_tiles.at[z], 3)
        wait_for(recv_sem.at[3], row_tiles, ROWS - 1)
        tiles = []
        for c in range(4):
            tile = None
            for zz in range(ROWS):
                shift = (2 * zz - 2 * c) % 8
                piece = row_tiles[zz]
                if shift:
                    piece = pltpu.roll(piece, shift, 0)
                tile = piece if tile is None else jnp.where(sub // 2 == zz, piece, tile)
            tiles.append(tile)
        for u in range(2):
            both = jnp.concatenate(tiles[2 * u : 2 * u + 2], axis=0).astype(BF16)
            wide[u] = both
            stream_all[j, u] = both
        late = jnp.where(j < 7, 0, 1)
        for peer in peers:
            pltpu.make_async_remote_copy(
                src_ref=wide, dst_ref=stream_all.at[j], send_sem=send_sem.at[4], recv_sem=stream_sem.at[late],
                device_id=plane + peer, device_id_type=LOGICAL,
            ).start()

    for copy in weights[2:4]:
        copy.wait()
    squares = jnp.zeros((8, 128), F32)
    gate_proj = up_proj = jnp.zeros((8, LOCAL_FF), F32)
    for g in range(2):
        low = 7 * g
        owner = jnp.logical_and(reducer, jnp.logical_and(own_chip >= low, own_chip < low + 7))

        @pl.when(owner)
        def _():
            wait_for(stream_sem.at[g], stream_all, 6)

        @pl.when(jnp.logical_not(owner))
        def _():
            wait_for(stream_sem.at[g], stream_all, 7)

        parts = stream_all[low : low + 7].astype(F32)
        tiles = [parts[t // 4, (t // 2) % 2, 8 * (t % 2) : 8 * (t % 2) + 8] for t in range(28)]
        for tile in tiles:
            squares = squares + tile * tile
        cols = pl.ds(3584 * g, 3584)
        stream = jnp.concatenate(tiles, axis=1)
        wide_stream[:, cols] = stream
        scaled = (stream * gain[cols].astype(F32).reshape(1, 3584)).astype(BF16)
        gate_proj = gate_proj + dot(scaled, wg[:, cols], ((1,), (1,)))
        up_proj = up_proj + dot(scaled, wu[:, cols], ((1,), (1,)))
    rstd = lax.rsqrt(jnp.sum(squares, axis=1, keepdims=True) * (1.0 / D) + 1e-06)
    gate_proj = gate_proj * rstd
    hidden = (gate_proj / (1.0 + jnp.exp(-gate_proj)) * (up_proj * rstd)).astype(BF16)
    weights[4].wait()
    own_half, in_half = lax.div(k, 16), lax.rem(k, 16)
    for own, first in enumerate((16 - 16 * own_half, 16 * own_half)):
        down = dot(hidden, wd[:, pl.ds(pl.multiple_of(first * OUT_COLS, 128), 3584)])
        down = jnp.concatenate([down, jnp.zeros((8, 128), F32)], axis=1)
        for p in range(16):
            tile, shift = divmod(OUT_COLS * p, 128)
            three = [down[:, 128 * (tile + i) : 128 * (tile + i + 1)] for i in range(3 if shift else 2)]
            if shift:
                turned = [pltpu.roll(t, 128 - shift, 1) for t in three]
                two = [jnp.where(lane < 128 - shift, turned[i], turned[i + 1]) for i in range(2)]
            else:
                two = three
            down_out[first + p] = jnp.concatenate(two, axis=0).astype(BF16)
        for d in range(own, 16):
            peer = first + lax.rem(in_half + d, 16)
            send(down_out.at[peer], down_in.at[k], 5, plane + peer)
    down_in[k] = down_out[k]

    own_tile = lax.div(7 * k, 4)
    wide_stream[:, pl.ds(D, 512)] = jnp.zeros((8, 512), F32)
    own_stream = wide_stream[:, pl.ds(pl.multiple_of(own_tile * 128, 128), 512)]
    own_stream = pltpu.roll(own_stream, lax.rem(512 - (OUT_COLS * k - 128 * own_tile), 512), 1)[:, :256]

    wait_for(recv_sem.at[5], down_in, KV - 1)
    mine = jnp.sum(down_in[...].astype(F32), axis=0)
    last_own[...] = mine
    last_in[z] = mine
    send_row(last_own, last_in.at[z], 6)
    wait_for(recv_sem.at[6], last_in, ROWS - 1)
    final = jnp.sum(last_in[...], axis=0)
    result = jnp.concatenate([final[0:8], final[8:16]], axis=1) + own_stream
    own = result[0:2]
    for zz in range(1, ROWS):
        own = jnp.where(z == zz, result[2 * zz : 2 * zz + 2], own)
    out_ref[...] = own[:, :OUT_COLS]

    for i, buffer in ((1, part_in), (5, down_in)):
        wait_for(send_sem.at[i], buffer, KV - 1)
    wait_for(send_sem.at[6], last_in, ROWS - 1)

    @pl.when(reducer)
    def _():
        wait_for(send_sem.at[2], attn_out, REDUCERS - 1)
        wait_for(send_sem.at[3], row_tiles, ROWS - 1)
        sent = s.at[0, pl.ds(0, 16), pl.ds(0, 128 * (KV - 1))]
        pltpu.make_async_copy(sent, sent, send_sem.at[4]).wait()

    @pl.when(jnp.logical_not(reducer))
    def _():
        wait_for(send_sem.at[2], attn_out, REDUCERS)


def body(query, latent_cache, new_latent, lengths, w_uv, w_o, hidden_in, norm_gain, w_gate, w_up, w_down):
    anywhere = pl.BlockSpec(memory_space=pl.ANY)
    vmem = pltpu.VMEM
    return pl.pallas_call(
        kernel,
        out_shape=jax.ShapeDtypeStruct((HERE, OUT_COLS), F32),
        in_specs=[anywhere] * 3 + [pl.BlockSpec(memory_space=pltpu.SMEM)] + [anywhere] * 7,
        out_specs=pl.BlockSpec(memory_space=vmem),
        scratch_shapes=[
            vmem((HERE, QK, HEADS), BF16),
            vmem((HERE, QK, SPAN), BF16),
            vmem((HERE, QK), BF16),
            vmem((4, LATENT, HEAD_DIM), BF16),
            vmem((4 * HEAD_DIM, D), BF16),
            vmem((HERE, D), BF16),
            vmem((D,), BF16),
            vmem((LOCAL_FF, D), BF16),
            vmem((LOCAL_FF, D), BF16),
            vmem((LOCAL_FF, D), BF16),
            vmem((HERE, HEADS, QK), BF16),
            vmem((HERE, HEADS, SPAN), F32),
            vmem((HERE, HEADS, SPAN), BF16),
            vmem((HERE, LATENT, HEADS), F32),
            vmem((REDUCERS, 8, 128), F32),
            vmem((KV // 2, 2, HERE + 1, 16, 128), BF16),
            vmem((KV, HERE + 1, 16, 128), BF16),
            vmem((REDUCERS, 8, 128), F32),
            vmem((KV, 8, 128), F32),
            vmem((ROWS, 8, 128), F32),
            vmem((8, 128), F32),
            vmem((REDUCERS, 2, 16, 128), BF16),
            vmem((2, 16, 128), BF16),
            vmem((KV, 16, 128), BF16),
            vmem((KV, 16, 128), BF16),
            vmem((16, 128), F32),
            vmem((ROWS, 16, 128), F32),
            vmem((8, D + 512), F32),
            pltpu.SemaphoreType.DMA((9,)),
            pltpu.SemaphoreType.DMA((HERE, CHUNKS)),
            pltpu.SemaphoreType.DMA((7,)),
            pltpu.SemaphoreType.DMA((7,)),
            pltpu.SemaphoreType.DMA((2,)),
        ],
        compiler_params=pltpu.CompilerParams(
            collective_id=0, has_side_effects=True, vmem_limit_bytes=60 * 1024 * 1024
        ),
    )(
        jnp.swapaxes(query, 1, 2),
        jnp.swapaxes(latent_cache, 1, 2),
        new_latent,
        lengths,
        w_uv,
        w_o,
        hidden_in,
        norm_gain,
        w_gate.T,
        w_up.T,
        w_down,
    )


def solution(mesh):
    placed = (
        P("row", None, None),
        P("row", "kv", None),
        P("row", None),
        P("row"),
        P("kv", None, None),
        P("kv", None),
        P("row", None),
        P(),
        P(None, ("row", "kv")),
        P(None, ("row", "kv")),
        P(("row", "kv"), None),
    )
    return jax.shard_map(body, mesh=mesh, in_specs=placed, out_specs=P("row", "kv"), check_vma=False)
```

```python
import jax
import jax.numpy as jnp
from jax import lax
from jax.experimental import pallas as pl
from jax.experimental.pallas import tpu as pltpu
from jax.sharding import PartitionSpec as P

LOGICAL = pl.DeviceIdType.LOGICAL
F32, BF16 = jnp.float32, jnp.bfloat16

HEADS, LATENT, ROPE, HEAD_DIM, QK = 128, 512, 64, 128, 576
D, LOCAL_FF, SPAN = 7168, 144, 5120
KV, ROWS, HERE = 32, 4, 2
OUT_COLS = D // KV
CHUNK = 1024
BLOCK = 256
CHUNKS = SPAN // CHUNK
REDUCERS = 14
LOG2E = 1.4426950408889634
SCALE2 = LOG2E * (HEAD_DIM + ROPE) ** -0.5
NEG_FILL = -1e30


def dot(a, b, dims=((1,), (0,))):
    return lax.dot_general(a, b, (dims, ((), ())), preferred_element_type=F32)


def kernel(
    q_hbm, cache_hbm, new_hbm, lengths_ref, uv_hbm, wo_hbm, hid_hbm, gain_hbm, gate_hbm, up_hbm, down_hbm,
    out_ref,
    qt, kt, new, uv, wo, hid_in, gain, wg, wu, wd,
    q, s, w, acc, hid_tiles,
    part_out, part_in, attn_out, attn_in, row_tiles, stream_own, stream_all, wide,
    down_out, down_in, last_own, last_in, wide_stream,
    in_sem, cache_sem, send_sem, recv_sem, stream_sem,
):
    k = lax.axis_index("kv")
    z = lax.axis_index("row")

    small = [
        pltpu.make_async_copy(src, dst, in_sem.at[i])
        for i, (src, dst) in enumerate(((q_hbm, qt), (new_hbm, new), (hid_hbm, hid_in), (gain_hbm, gain)))
    ]
    for copy in small:
        copy.start()
    cache = [
        [
            pltpu.make_async_copy(
                cache_hbm.at[r, :, pl.ds(c * CHUNK, CHUNK)], kt.at[r, :, pl.ds(c * CHUNK, CHUNK)], cache_sem.at[r, c]
            )
            for c in range(CHUNKS)
        ]
        for r in range(HERE)
    ]
    for r in range(HERE):
        for c in range(CHUNKS):
            cache[r][c].start()
    weights = [
        pltpu.make_async_copy(src, dst, in_sem.at[4 + i])
        for i, (src, dst) in enumerate(((uv_hbm, uv), (wo_hbm, wo), (gate_hbm, wg), (up_hbm, wu), (down_hbm, wd)))
    ]

    barrier = pltpu.get_barrier_semaphore()

    plane = z * KV
    own_chip, own_core = lax.div(k, 2), lax.rem(k, 2)
    xs = [4 * lax.rem(lax.div(own_chip, 4) + d, 4) for d in range(4)]
    ys = [lax.rem(lax.rem(own_chip, 4) + d, 4) for d in range(4)]
    cores = [own_core, 1 - own_core]
    offsets = sorted(((dx, dy) for dx in range(4) for dy in range(4)), key=lambda o: -min(o[0], 4 - o[0]) - min(o[1], 4 - o[1]))
    chips = [xs[dx] + ys[dy] for dx, dy in offsets]
    peers = [2 * chip + core for chip in chips for core in cores]
    del peers[-2]
    row_peers = [lax.rem(z + d, ROWS) * KV + k for d in (2, 1, 3)]
    for peer in [plane + p for p in peers] + row_peers:
        pl.semaphore_signal(barrier, inc=1, device_id=peer, device_id_type=LOGICAL)

    def send(src, dst, lane, device):
        pltpu.make_async_remote_copy(
            src_ref=src, dst_ref=dst, send_sem=send_sem.at[lane], recv_sem=recv_sem.at[lane],
            device_id=device, device_id_type=LOGICAL,
        ).start()

    def send_kv(src, dst, lane):
        for peer in peers:
            send(src(peer), dst, lane, plane + peer)

    def send_row(src, dst, lane):
        for peer in row_peers:
            send(src, dst, lane, peer)

    def wait_for(sem, buffer, count):
        span = buffer.at[pl.ds(0, count)]
        pltpu.make_async_copy(span, span, sem).wait()

    sub = lax.broadcasted_iota(jnp.int32, (8, 128), 0)
    lane = lax.broadcasted_iota(jnp.int32, (8, 128), 1)

    small[0].wait()
    for r in range(HERE):
        q[r] = qt[r].astype(F32).T.astype(BF16)

    def packed(rows, j):
        base = 512 * j
        tile = rows[:, base : base + 128]
        for c in range(1, 4):
            tile = jnp.where(sub // 2 == c, rows[:, base + 128 * c : base + 128 * (c + 1)], tile)
        return tile

    position = lax.broadcasted_iota(jnp.int32, (1, BLOCK), 1) + k * SPAN

    def scores(r, c):
        cache[r][c].wait()
        most = None
        for first in range(c * CHUNK, (c + 1) * CHUNK, BLOCK):
            cols = pl.ds(first, BLOCK)
            raw = dot(q[r], kt[r, :, cols]) * SCALE2
            raw = jnp.where(position + first < lengths_ref[r], raw, NEG_FILL)
            s[r, :, cols] = raw
            for part in range(0, BLOCK, 128):
                piece = raw[:, part : part + 128]
                most = piece if most is None else jnp.maximum(most, piece)
        return most

    def weigh(r, c, top):
        cols = pl.ds(c * CHUNK, CHUNK)
        value = jnp.exp2(s[r, :, cols] - top)
        w[r, :, cols] = value.astype(BF16)
        added = value[:, :128]
        for part in range(128, CHUNK, 128):
            added = added + value[:, part : part + 128]
        return added

    def highest(r, parts):
        most = parts[0]
        for part in parts[1:]:
            most = jnp.maximum(most, part)
        new_score = jnp.sum(q[r].astype(F32) * new[r : r + 1, :].astype(F32), axis=1, keepdims=True) * SCALE2
        return new_score, jnp.maximum(jnp.max(most, axis=1, keepdims=True), new_score)

    def summed(parts):
        added = parts[0]
        for part in parts[1:]:
            added = added + part
        return jnp.sum(added, axis=1, keepdims=True)

    parts = [scores(0, c) for c in range(CHUNKS)]
    small[1].wait()
    new0, top0 = highest(0, parts)
    weights[0].start()
    weights[1].start()
    parts, sums = [], []
    for c in range(CHUNKS):
        parts.append(scores(1, c))
        sums.append(weigh(0, c, top0))
    for copy in weights[2:]:
        copy.start()
    new1, top1 = highest(1, parts)
    new_score, top = [new0, new1], [top0, top1]
    total = [summed(sums), summed([weigh(1, c, top1) for c in range(CHUNKS)])]
    for r in range(HERE):
        acc[r] = dot(kt[r, :LATENT, :], w[r], ((1,), (1,)))

    half = lax.broadcasted_iota(jnp.int32, (16, 8, 128), 1) < 4
    left = lax.broadcasted_iota(jnp.int32, (HEADS, 128), 1) < 64
    wide_zero = jnp.zeros((HEADS, 128), F32)

    def share(first, second):
        t0, t1 = first.reshape(16, 8, 128), second.reshape(16, 8, 128)
        return jnp.where(half, t0, pltpu.roll(t1, 4, 1)), jnp.where(half, pltpu.roll(t0, 4, 1), t1)

    def rounded(value):
        return value.astype(BF16).astype(F32)

    logs = []
    for r in range(HERE):
        own_new = jnp.where(k == 0, jnp.exp2(new_score[r] - top[r]), 0.0)
        norm = jnp.maximum(total[r] + own_new, 1e-30)
        log_total = top[r] + jnp.log(norm) * LOG2E
        high = rounded(log_total)
        middle = rounded(log_total - high)
        low = log_total - high - middle
        logs.append(share(jnp.where(left, high, middle), jnp.where(left, low, wide_zero)))
        mine = (acc[r].T + own_new * new[r : r + 1, :LATENT].astype(F32)) * (1.0 / norm)
        quarters = [mine[:, 128 * c : 128 * c + 128] for c in range(4)]
        both = [share(quarters[2 * u], quarters[2 * u + 1]) for u in range(2)]
        for core in range(2):
            part_out[:, core, r] = jnp.concatenate([both[0][core], both[1][core]], axis=1).astype(BF16)
    for core in range(2):
        part_out[:, core, HERE] = jnp.concatenate([logs[0][core], logs[1][core]], axis=1).astype(BF16)
    pl.semaphore_wait(barrier, KV - 1 + ROWS - 1)
    send_kv(lambda peer: part_out.at[lax.div(peer, 2), lax.rem(peer, 2)], part_in.at[k], 1)
    part_in[k] = part_out[own_chip, own_core]

    for copy in small[2:]:
        copy.wait()
    hid_f = hid_in[...].astype(F32)
    hid_rows = jnp.where(lax.broadcasted_iota(jnp.int32, (8, D), 0) % 2 == 0, hid_f[0:1], hid_f[1:2])

    for j in range(REDUCERS):
        hid_tiles[j] = packed(hid_rows, j)

    wait_for(recv_sem.at[1], part_in, KV - 1)
    weights[0].wait()
    att = []
    for r in range(HERE):
        log_parts = part_in[:, HERE, 8 * r : 8 * r + 8].astype(F32)
        log_parts = log_parts + pltpu.roll(log_parts, 64, 2)
        log_parts = log_parts + pltpu.roll(log_parts, 4, 1)
        factor = jnp.exp2(log_parts - jnp.max(log_parts, axis=0)[None])
        factor = factor * (1.0 / jnp.sum(factor, axis=0))[None]
        data = part_in[:, r].astype(F32)
        att.append([jnp.sum(data[:, 8 * u : 8 * u + 8] * factor, axis=0) for u in range(2)])
    pieces = []
    for c in range(4):
        lo, hi = att[0][c // 2], att[1][c // 2]
        if c % 2 == 0:
            pieces.append(jnp.where(sub < 4, lo, pltpu.roll(hi, 4, 0)))
        else:
            pieces.append(jnp.where(sub < 4, pltpu.roll(lo, 4, 0), hi))
    attended = jnp.concatenate(pieces, axis=1).astype(BF16)
    values = []
    for h in range(4):
        got = dot(attended, uv[h])
        values.append(jnp.where(sub % 2 == 0, got[h : h + 1], got[4 + h : 5 + h]))
    head_values = jnp.concatenate(values, axis=1).astype(BF16)
    weights[1].wait()
    for low in (0, 7):
        partial = dot(head_values, wo[:, 512 * low : 512 * (low + 7)])
        for j in range(7):
            attn_out[low + j] = packed(partial, j)
        for chip in chips:

            @pl.when(jnp.logical_and(jnp.logical_and(chip >= low, chip < low + 7), k != 2 * chip))
            def _(chip=chip):
                send(attn_out.at[chip], attn_in.at[k], 2, plane + 2 * chip)

    reducer = jnp.logical_and(k % 2 == 0, k < 2 * REDUCERS)

    @pl.when(reducer)
    def _():
        j = own_chip
        attn_in[k] = attn_out[j]
        own_hid = hid_tiles[j]
        wait_for(recv_sem.at[2], attn_in, KV - 1)
        mine = (jnp.sum(attn_in[...], axis=0) + own_hid).astype(BF16).astype(F32)
        row_tiles[z] = mine
        stream_own[...] = mine
        send_row(stream_own, row_tiles.at[z], 3)
        wait_for(recv_sem.at[3], row_tiles, ROWS - 1)
        tiles = []
        for c in range(4):
            tile = None
            for zz in range(ROWS):
                shift = (2 * zz - 2 * c) % 8
                piece = row_tiles[zz]
                if shift:
                    piece = pltpu.roll(piece, shift, 0)
                tile = piece if tile is None else jnp.where(sub // 2 == zz, piece, tile)
            tiles.append(tile)
        for u in range(2):
            both = jnp.concatenate(tiles[2 * u : 2 * u + 2], axis=0).astype(BF16)
            wide[u] = both
            stream_all[j, u] = both
        late = jnp.where(j < 7, 0, 1)
        for peer in peers:
            pltpu.make_async_remote_copy(
                src_ref=wide, dst_ref=stream_all.at[j], send_sem=send_sem.at[4], recv_sem=stream_sem.at[late],
                device_id=plane + peer, device_id_type=LOGICAL,
            ).start()

    for copy in weights[2:4]:
        copy.wait()
    squares = jnp.zeros((8, 128), F32)
    gate_proj = up_proj = jnp.zeros((LOCAL_FF, 8), F32)
    for g in range(2):
        low = 7 * g
        owner = jnp.logical_and(reducer, jnp.logical_and(own_chip >= low, own_chip < low + 7))

        @pl.when(owner)
        def _():
            wait_for(stream_sem.at[g], stream_all, 6)

        @pl.when(jnp.logical_not(owner))
        def _():
            wait_for(stream_sem.at[g], stream_all, 7)

        parts = stream_all[low : low + 7].astype(F32)
        tiles = [parts[t // 4, (t // 2) % 2, 8 * (t % 2) : 8 * (t % 2) + 8] for t in range(28)]
        for tile in tiles:
            squares = squares + tile * tile
        cols = pl.ds(3584 * g, 3584)
        stream = jnp.concatenate(tiles, axis=1)
        wide_stream[:, cols] = stream
        scaled = (stream * gain[cols].astype(F32).reshape(1, 3584)).astype(BF16)
        gate_proj = gate_proj + dot(wg[:, cols], scaled, ((1,), (1,)))
        up_proj = up_proj + dot(wu[:, cols], scaled, ((1,), (1,)))
    rstd = lax.rsqrt(jnp.sum(squares, axis=1, keepdims=True) * (1.0 / D) + 1e-06)
    gate_proj, up_proj = gate_proj.T * rstd, up_proj.T * rstd
    hidden = (gate_proj / (1.0 + jnp.exp(-gate_proj)) * up_proj).astype(BF16)
    weights[4].wait()
    own_half, in_half = lax.div(k, 16), lax.rem(k, 16)
    for own, first in enumerate((16 - 16 * own_half, 16 * own_half)):
        down = dot(hidden, wd[:, pl.ds(pl.multiple_of(first * OUT_COLS, 128), 3584)])
        down = jnp.concatenate([down, jnp.zeros((8, 128), F32)], axis=1)
        for p in range(16):
            tile, shift = divmod(OUT_COLS * p, 128)
            three = [down[:, 128 * (tile + i) : 128 * (tile + i + 1)] for i in range(3 if shift else 2)]
            if shift:
                turned = [pltpu.roll(t, 128 - shift, 1) for t in three]
                two = [jnp.where(lane < 128 - shift, turned[i], turned[i + 1]) for i in range(2)]
            else:
                two = three
            down_out[first + p] = jnp.concatenate(two, axis=0).astype(BF16)
        for d in range(own, 16):
            peer = first + lax.rem(in_half + d, 16)
            send(down_out.at[peer], down_in.at[k], 5, plane + peer)
    down_in[k] = down_out[k]

    own_tile = lax.div(7 * k, 4)
    wide_stream[:, pl.ds(D, 512)] = jnp.zeros((8, 512), F32)
    own_stream = wide_stream[:, pl.ds(pl.multiple_of(own_tile * 128, 128), 512)]
    own_stream = pltpu.roll(own_stream, lax.rem(512 - (OUT_COLS * k - 128 * own_tile), 512), 1)[:, :256]

    wait_for(recv_sem.at[5], down_in, KV - 1)
    mine = jnp.sum(down_in[...].astype(F32), axis=0)
    last_own[...] = mine
    last_in[z] = mine
    send_row(last_own, last_in.at[z], 6)
    wait_for(recv_sem.at[6], last_in, ROWS - 1)
    final = jnp.sum(last_in[...], axis=0)
    result = jnp.concatenate([final[0:8], final[8:16]], axis=1) + own_stream
    own = result[0:2]
    for zz in range(1, ROWS):
        own = jnp.where(z == zz, result[2 * zz : 2 * zz + 2], own)
    out_ref[...] = own[:, :OUT_COLS]

    for i, buffer in ((1, part_in), (5, down_in)):
        wait_for(send_sem.at[i], buffer, KV - 1)
    wait_for(send_sem.at[6], last_in, ROWS - 1)

    @pl.when(reducer)
    def _():
        wait_for(send_sem.at[2], attn_out, REDUCERS - 1)
        wait_for(send_sem.at[3], row_tiles, ROWS - 1)
        sent = s.at[0, pl.ds(0, 16), pl.ds(0, 128 * (KV - 1))]
        pltpu.make_async_copy(sent, sent, send_sem.at[4]).wait()

    @pl.when(jnp.logical_not(reducer))
    def _():
        wait_for(send_sem.at[2], attn_out, REDUCERS)


def body(query, latent_cache, new_latent, lengths, w_uv, w_o, hidden_in, norm_gain, w_gate, w_up, w_down):
    anywhere = pl.BlockSpec(memory_space=pl.ANY)
    vmem = pltpu.VMEM
    return pl.pallas_call(
        kernel,
        out_shape=jax.ShapeDtypeStruct((HERE, OUT_COLS), F32),
        in_specs=[anywhere] * 3 + [pl.BlockSpec(memory_space=pltpu.SMEM)] + [anywhere] * 7,
        out_specs=pl.BlockSpec(memory_space=vmem),
        scratch_shapes=[
            vmem((HERE, QK, HEADS), BF16),
            vmem((HERE, QK, SPAN), BF16),
            vmem((HERE, QK), BF16),
            vmem((4, LATENT, HEAD_DIM), BF16),
            vmem((4 * HEAD_DIM, D), BF16),
            vmem((HERE, D), BF16),
            vmem((D,), BF16),
            vmem((LOCAL_FF, D), BF16),
            vmem((LOCAL_FF, D), BF16),
            vmem((LOCAL_FF, D), BF16),
            vmem((HERE, HEADS, QK), BF16),
            vmem((HERE, HEADS, SPAN), F32),
            vmem((HERE, HEADS, SPAN), BF16),
            vmem((HERE, LATENT, HEADS), F32),
            vmem((REDUCERS, 8, 128), F32),
            vmem((KV // 2, 2, HERE + 1, 16, 128), BF16),
            vmem((KV, HERE + 1, 16, 128), BF16),
            vmem((REDUCERS, 8, 128), F32),
            vmem((KV, 8, 128), F32),
            vmem((ROWS, 8, 128), F32),
            vmem((8, 128), F32),
            vmem((REDUCERS, 2, 16, 128), BF16),
            vmem((2, 16, 128), BF16),
            vmem((KV, 16, 128), BF16),
            vmem((KV, 16, 128), BF16),
            vmem((16, 128), F32),
            vmem((ROWS, 16, 128), F32),
            vmem((8, D + 512), F32),
            pltpu.SemaphoreType.DMA((9,)),
            pltpu.SemaphoreType.DMA((HERE, CHUNKS)),
            pltpu.SemaphoreType.DMA((7,)),
            pltpu.SemaphoreType.DMA((7,)),
            pltpu.SemaphoreType.DMA((2,)),
        ],
        compiler_params=pltpu.CompilerParams(
            collective_id=0, has_side_effects=True, vmem_limit_bytes=60 * 1024 * 1024
        ),
    )(
        jnp.swapaxes(query, 1, 2),
        jnp.swapaxes(latent_cache, 1, 2),
        new_latent,
        lengths,
        w_uv,
        w_o,
        hidden_in,
        norm_gain,
        w_gate.T,
        w_up.T,
        w_down,
    )


def solution(mesh):
    placed = (
        P("row", None, None),
        P("row", "kv", None),
        P("row", None),
        P("row"),
        P("kv", None, None),
        P("kv", None),
        P("row", None),
        P(),
        P(None, ("row", "kv")),
        P(None, ("row", "kv")),
        P(("row", "kv"), None),
    )
    return jax.shard_map(body, mesh=mesh, in_specs=placed, out_specs=P("row", "kv"), check_vma=False)
```
